256 devices in a mesh: ctx: 32 (over y, x, core), tp: 4 (over z_hi), dp: 2 (over z_lo).
Axes of the slice: x: 4, y: 4, z: 8 (z_hi: 4, z_lo: 2; z = z_hi * 2 + z_lo), core: 2. Of those that a mesh axis runs over, the one named last changes fastest.
Arguments:
- residual: bfloat16 [2, 4096, 2048], P('dp', 'ctx', 'tp'), may hold values from -3 to 3
- queries: bfloat16 [2, 4096, 2048], P('dp', 'ctx', 'tp'), may hold values from -6 to 6
- attn_keys: bfloat16 [2, 4096, 2048], P('dp', 'ctx', 'tp'), may hold values from -6 to 6
- attn_values: bfloat16 [2, 4096, 2048], P('dp', 'ctx', 'tp'), may hold values from -24 to 24
- gate_table: bfloat16 [1000, 2048], P(None, 'tp'), may hold values from 0.19921875 to 1.796875
- timesteps: int32 [2], P('dp'), may hold values from 0 to 999
- enc_feats: bfloat16 [2, 1536, 1536], P('dp', 'ctx', 'tp'), may hold values from -6 to 6
- tap_rows: int32 [2, 4096, 4], P('dp', 'ctx'), may hold values from 0 to 1535
- tap_weights: float32 [2, 4096, 4], P('dp', 'ctx'), may hold values from 0.1 to 1
- proj_in: bfloat16 [2048, 2048], P('tp'), may hold values from -0.125 to 0.125
- proj_out: bfloat16 [2048, 1536], P('tp'), may hold values from -0.125 to 0.125
Outputs:
- d_hidden: bfloat16 [2, 4096, 2048], P('dp', 'ctx', 'tp')
- grad_proj_in: float32 [2048, 2048], P('tp', 'ctx')
- grad_proj_out: float32 [2048, 1536], P('tp', 'ctx')
The draws below stay inside these ranges and needn't reach their ends.
All inputs are finite; a program needn't handle non-finite values.
Results may differ from the reference program's by a relative error of at most 0.025.
Values may be sent and summed in bfloat16 or wider, within the bound.
A program may use at most 64 MiB of HBM per device.

```python
import math
import jax
import jax.numpy as jnp
from jax import lax

D = 2048
HEADS = 16
HD = 128
HID = 2048
ZD = 1536
TSTEPS = 1000
SEQ = 4096
ENC_ROWS = 1536
IMAGES = 2


def draw_queries(key, part):
    key = jax.random.fold_in(key, 3)
    full_shape = (IMAGES, SEQ, D)
    values = 1.5 * jax.random.truncated_normal(key, -4.0, 4.0, full_shape, jnp.float32)
    return values.astype(jnp.bfloat16)


def draw_attn_keys(key, part):
    key = jax.random.fold_in(key, 5)
    full_shape = (IMAGES, SEQ, D)
    values = 1.5 * jax.random.truncated_normal(key, -4.0, 4.0, full_shape, jnp.float32)
    return values.astype(jnp.bfloat16)


def with_ends(drawn, stream_key, smallest, high):
    dims = drawn.shape
    spot = [jax.random.randint(jax.random.fold_in(stream_key, axis), (), 0, dims[axis]) for axis in range(len(dims))]
    drawn = drawn.at[tuple(spot)].set(smallest)
    longest = dims.index(max(dims))
    spot[longest] = (spot[longest] + 1) % dims[longest]
    return drawn.at[tuple(spot)].set(high)


def block_scale(own_key, extent, cuts, least, largest):
    level, own = 1.0, jax.random.fold_in(own_key, 6)
    for dim, parts in cuts:
        heights = jnp.exp(jax.random.uniform(jax.random.fold_in(own, dim), (parts,), jnp.float32, least / len(cuts), largest / len(cuts)))
        level = level * jnp.repeat(heights, extent[dim] // parts).reshape([-1 if axis == dim else 1 for axis in range(len(extent))])
    return level


def noise(stream_key, extent, scale, limit, split=(), kind=jnp.bfloat16):
    factor_of = block_scale(stream_key, extent, split, -0.22, 0.18) if split else 1.0
    drawn = jax.random.normal(stream_key, extent, jnp.float32) * scale * factor_of
    return jnp.minimum(jnp.maximum(drawn, -limit), limit).astype(kind)


def setup_inputs(seed: int = 0) -> dict:
    key_of = jax.random.split(jax.random.key(seed), 12)
    residual = noise(key_of[0], (IMAGES, SEQ, D), 0.5, 3.0, ((0, 2), (1, 32), (2, 4)))
    queries = draw_queries(jax.random.fold_in(key_of[11], 71), 0)
    attn_keys = draw_attn_keys(jax.random.fold_in(key_of[11], 71), 0)
    attn_values = noise(key_of[3], (IMAGES, SEQ, D), 4.0, 24.0, ((0, 2), (1, 32), (2, 4)))
    gate_table = jnp.clip(0.19921875 + 1.5976562 * jax.random.uniform(key_of[4], (TSTEPS, D), jnp.float32) ** block_scale(key_of[4], (TSTEPS, D), ((1, 4),), -0.2, 0.2), 0.19921875, 1.796875).astype(jnp.bfloat16)
    timesteps = jax.random.randint(key_of[5], (IMAGES,), 0, TSTEPS).astype(jnp.int32)
    enc_feats = noise(key_of[6], (IMAGES, ENC_ROWS, ZD), 1.0, 6.0, ((0, 2), (1, 32), (2, 4)))
    tap_rows = with_ends(jax.random.randint(key_of[7], (IMAGES, SEQ, 4), 0, ENC_ROWS), jax.random.fold_in(key_of[7], 1), 0, ENC_ROWS - 1).astype(jnp.int32)
    tap_weights = jnp.clip(jnp.exp(math.log(1.0) - 2.3025851 * jax.random.uniform(key_of[8], (IMAGES, SEQ, 4), jnp.float32) ** block_scale(key_of[8], (IMAGES, SEQ, 4), ((0, 2), (1, 32)), -0.2, 0.2)), 0.1, 1.0)
    proj_in = noise(key_of[9], (D, HID), D ** -0.5, 0.125, ((0, 4),))
    proj_out = noise(key_of[10], (HID, ZD), HID ** -0.5, 0.125, ((0, 4),))
    return {"residual": residual, "queries": queries, "attn_keys": attn_keys, "attn_values": attn_values, "gate_table": gate_table, "timesteps": timesteps, "enc_feats": enc_feats, "tap_rows": tap_rows, "tap_weights": tap_weights, "proj_in": proj_in, "proj_out": proj_out}


eps = 1e-06
loss_scale = 4194304.0

def attend_image(query_img, key_img, value_img):
    query_heads = query_img.reshape(SEQ, HEADS, HD).transpose(1, 0, 2)
    key_heads = key_img.reshape(SEQ, HEADS, HD).transpose(1, 0, 2)
    value_heads = value_img.reshape(SEQ, HEADS, HD).transpose(1, 0, 2)

    def one_head(operands):
        query_one, key_one, value_one = operands
        scores = jnp.dot(query_one, key_one.T, preferred_element_type=jnp.float32) * HD ** (-0.5)
        row_max = lax.optimization_barrier(jnp.max(scores, axis=1, keepdims=True))
        expo = jnp.exp(scores - row_max)
        denominator = lax.optimization_barrier(jnp.sum(expo, axis=1, keepdims=True))
        weights = expo.astype(jnp.bfloat16)
        return jnp.dot(weights, value_one, preferred_element_type=jnp.float32) / denominator
    outputs = lax.map(one_head, (query_heads, key_heads, value_heads))
    return outputs.transpose(1, 0, 2).reshape(SEQ, D)

def silu_slope(inner):
    sigma = jax.nn.sigmoid(inner)
    return sigma * (1.0 + inner * (1.0 - sigma))

def reference(residual, queries, attn_keys, attn_values, gate_table, timesteps, enc_feats, tap_rows, tap_weights, proj_in, proj_out):
    gates = gate_table[timesteps].astype(jnp.float32)
    hidden_list = []
    target_list = []
    for image_index in range(IMAGES):
        attention = attend_image(queries[image_index], attn_keys[image_index], attn_values[image_index])
        hidden_img = residual[image_index].astype(jnp.float32) + gates[image_index][None, :] * attention
        hidden_list.append(hidden_img.astype(jnp.bfloat16))
        picked = enc_feats[image_index][tap_rows[image_index]].astype(jnp.float32)
        tap_norm = tap_weights[image_index] / lax.optimization_barrier(jnp.sum(tap_weights[image_index], axis=1, keepdims=True))
        target_list.append(lax.optimization_barrier(jnp.sum(tap_norm[:, :, None] * picked, axis=1)))
    hidden = jnp.concatenate(hidden_list, axis=0)
    target = jnp.concatenate(target_list, axis=0)
    inner = jnp.dot(hidden, proj_in, preferred_element_type=jnp.float32)
    activation = jax.nn.silu(inner).astype(jnp.bfloat16)
    projected = jnp.dot(activation, proj_out, preferred_element_type=jnp.float32)
    norm_p = jnp.sqrt(lax.optimization_barrier(jnp.sum(projected * projected, axis=1, keepdims=True)) + eps)
    norm_t = jnp.sqrt(lax.optimization_barrier(jnp.sum(target * target, axis=1, keepdims=True)) + eps)
    cosine = lax.optimization_barrier(jnp.sum(projected * target, axis=1, keepdims=True)) / (norm_p * norm_t)
    factor = loss_scale / (IMAGES * SEQ)
    grad_proj = (-factor * (target / (norm_p * norm_t) - cosine * projected / (norm_p * norm_p))).astype(jnp.bfloat16)
    grad_act = jnp.dot(grad_proj, proj_out.T, preferred_element_type=jnp.float32)
    grad_inner = (grad_act * silu_slope(inner)).astype(jnp.bfloat16)
    d_hidden = jnp.dot(grad_inner, proj_in.T, preferred_element_type=jnp.float32).astype(jnp.bfloat16)
    grad_proj_in = jnp.dot(hidden.T, grad_inner, preferred_element_type=jnp.float32)
    grad_proj_out = jnp.dot(activation.T, grad_proj, preferred_element_type=jnp.float32)
    return (d_hidden.reshape(IMAGES, SEQ, D), grad_proj_in, grad_proj_out)
```

```python
import functools
import math

import jax
import jax.numpy as jnp
from jax import lax
from jax.experimental import pallas as pl
from jax.experimental.pallas import tpu as pltpu
from jax.sharding import PartitionSpec as P

HD = 128
TOK = 128
eps = 1e-06
loss_scale = 4194304.0
ALL_TOKENS = 8192
BF = jnp.bfloat16
F32 = jnp.float32
MESH = pl.DeviceIdType.MESH
VMEM = pltpu.VMEM


def dot(a, b, ca, cb):
    return lax.dot_general(a, b, (((ca,), (cb,)), ((), ())), preferred_element_type=F32)


def kernel(
    res, q_in, k_in, v_in, gate_in, step, enc, tap_rows, tap_w, win_in, wout_in,
    d_out, gin_out, gout_out,
    qkv, gate, win, wout, encb, osend, ssend, orecv, srecv,
    tgs, tgt, hid, h2, isend, irecv, inner, act, a2, psend, precv, g2, gi2, dacc,
    p1a, p1b, r1a, r1b, s1a, s1b, t1a, t1b, f1, e1,
    p2a, p2b, r2a, r2b, s2a, s2b, t2a, t2b, f2, e2,
    load_sem, qkv_s, qkv_r, enc_s, enc_r, o_s, o_r, st_s, st_r, tg_s, tg_r,
    mate_s, mate_r, i_s, i_r, p_s, p_r, g_s, g_r, gi_s, gi_r, mg_s, mg_r,
    red_s, red_r,
):
    ctx = lax.axis_index("ctx")
    t = lax.axis_index("tp")
    dp = lax.axis_index("dp")
    c = lax.rem(ctx, 2)
    x = lax.rem(lax.div(ctx, 2), 4)
    y = lax.div(ctx, 8)
    me = x * 2 + c
    mine = y * 2 + c

    def at(yy, xx, cc, tt=None, dd=None):
        return {
            "ctx": (yy * 4 + xx) * 2 + cc,
            "tp": t if tt is None else tt,
            "dp": dp if dd is None else dd,
        }

    def up(v, d):
        return lax.rem(v + d, 4)

    mate = at(y, x, 1 - c)
    zpeer = {d: at(y, x, c, tt=up(t, d)) for d in (1, 2, 3)}
    xpeer = {d: at(y, up(x, d), c) for d in (1, 2, 3)}
    ypeer = {d: at(up(y, d), x, c) for d in (1, 2, 3)}

    def send(src, dst, ss, rs, dev):
        cp = pltpu.make_async_remote_copy(
            src_ref=src, dst_ref=dst, send_sem=ss, recv_sem=rs, device_id=dev, device_id_type=MESH
        )
        cp.start()

    def wait(ref, sem):
        pltpu.make_async_copy(ref, ref, sem).wait()

    loads = [
        pltpu.make_async_copy(win_in, win, load_sem.at[0]),
        pltpu.make_async_copy(wout_in, wout, load_sem.at[1]),
        pltpu.make_async_copy(gate_in, gate, load_sem.at[2]),
    ]

    bar = pltpu.get_barrier_semaphore()
    partners = [at(y, up(x, d), cc) for d in (1, 2, 3) for cc in (0, 1)]
    partners += [at(up(y, d), x, cc) for d in (1, 2, 3) for cc in (0, 1)]
    partners += [mate] + [zpeer[d] for d in (1, 2, 3)]
    partners += [at(y, x, cc, dd=1 - dp) for cc in (0, 1)]
    for p in partners:
        pl.semaphore_signal(bar, inc=1, device_id=p, device_id_type=MESH)
    pl.semaphore_wait(bar, len(partners))

    def cols(cc, j):
        return pl.ds(pl.multiple_of(cc * 256 + j * 128, 128), 128)

    for j in (0, 1):
        for n, src, axis in ((1, k_in, 0), (0, q_in, 1), (2, v_in, 0)):
            ss, rs = qkv_s.at[j, n], qkv_r.at[j, n]
            slot = me if axis == 1 else mine
            for d in (2, 1, 3, 0):
                for e in (0, 1):
                    cc = lax.rem(c + e, 2)
                    dst = qkv.at[j, n, slot]
                    if d == 0 and e == 0:
                        pltpu.make_async_copy(src.at[:, cols(cc, j)], dst, rs).start()
                        continue
                    dev = at(y, up(x, d), cc) if axis == 1 else at(up(y, d), x, cc)
                    send(src.at[:, cols(cc, j)], dst, ss, rs, dev)
    pltpu.make_async_copy(enc, encb.at[y, x, c], load_sem.at[3]).start()
    for d in (1, 2, 3):
        send(enc, encb.at[y, x, c], enc_s.at[0], enc_r.at[0], xpeer[d])
    for cp in loads:
        cp.start()

    scale = HD ** (-0.5) * math.log2(math.e)

    def head(j, carry):
        for n in (1, 0, 2):
            wait(qkv.at[j, n], qkv_r.at[j, n])
        keys = qkv[j, 1].reshape(8 * TOK, HD)
        vt = qkv[j, 2].reshape(8 * TOK, HD).T

        def block(it, carry2):
            xq = up(x, 1 + it)
            qb = qkv[j, 0, pl.ds(2 * xq, 2)].reshape(2 * TOK, HD)
            st = dot(keys, qb, 1, 1) * scale
            top = jnp.max(st, axis=0, keepdims=True)
            expo = jnp.exp2(st - top)
            total = jnp.sum(expo, axis=0, keepdims=True)
            ot = dot(vt, expo.astype(BF), 1, 0) / total
            lse = top + jnp.log2(total)
            for cc in (0, 1):
                osend[j, 2 * xq + cc] = ot[:, cc * TOK : (cc + 1) * TOK].astype(BF)
                ssend[2 * xq + cc, j] = jnp.broadcast_to(lse[:, cc * TOK : (cc + 1) * TOK], (8, TOK))
                own = jnp.logical_and(xq == x, cc == c)

                @pl.when(own)
                def _():
                    pltpu.make_async_copy(osend.at[j, 2 * xq + cc], orecv.at[x, c, j], o_r.at[j]).start()

                @pl.when(jnp.logical_not(own))
                def _():
                    send(osend.at[j, 2 * xq + cc], orecv.at[x, c, j], o_s.at[j], o_r.at[j], at(y, xq, cc))
            return carry2

        return lax.fori_loop(0, 4, block, carry)

    lax.fori_loop(0, 2, head, 0)
    for d in (2, 1, 3, 0):
        for cc in (0, 1):
            xq = up(x, d)
            if d == 0:
                @pl.when(cc == c)
                def _():
                    pltpu.make_async_copy(ssend.at[2 * xq + cc], srecv.at[x, c], st_r).start()

                @pl.when(cc != c)
                def _():
                    send(ssend.at[2 * xq + cc], srecv.at[x, c], st_s, st_r, at(y, xq, cc))
            else:
                send(ssend.at[2 * xq + cc], srecv.at[x, c], st_s, st_r, at(y, xq, cc))

    wait(enc, load_sem.at[3])
    wait(encb.at[0, pl.ds(0, 3), 0], enc_r.at[0])
    for d in (2, 1, 3):
        send(encb.at[y, :, c], encb.at[y, :, c], enc_s.at[1], enc_r.at[1], ypeer[d])
    for cp in loads:
        cp.wait()
    pick = (lax.broadcasted_iota(jnp.int32, (16, gate.shape[0]), 1) == step[0]).astype(F32).astype(BF)
    gate_row = dot(pick, gate[...], 1, 0)[0:1]
    base = res[...].astype(F32)

    for j in (0, 1):
        wait(orecv.at[:, :, j], o_r.at[j])
    wait(srecv, st_r)
    for cc in (0, 1):
        for j in (0, 1):
            lses = [srecv[i, cc, j, 0:1, :] for i in range(4)]
            top = jnp.maximum(jnp.maximum(lses[0], lses[1]), jnp.maximum(lses[2], lses[3]))
            ws = [jnp.exp2(v - top) for v in lses]
            inv = 1.0 / (ws[0] + ws[1] + ws[2] + ws[3])
            acc = sum(orecv[i, cc, j].astype(F32) * (ws[i] * inv) for i in range(4))
            lo = (2 * cc + j) * HD
            hid[:, lo : lo + HD] = (
                base[:, lo : lo + HD] + gate_row[:, lo : lo + HD] * acc.T
            ).astype(BF)

    half = pl.ds(pl.multiple_of(c * 256, 256), 256)
    other = pl.ds(pl.multiple_of((1 - c) * 256, 256), 256)

    def slab(tt):
        return pl.ds(pl.multiple_of(tt * 512, 512), 512)

    for d in (2, 1, 3):
        isend[d - 1] = dot(hid[...], win[:, slab(up(t, d))], 1, 0).astype(BF)
        send(isend.at[d - 1], irecv.at[d - 1], i_s, i_r, zpeer[d])
    inner[...] = dot(hid[...], win[:, slab(t)], 1, 0)
    h2[0:TOK] = hid[:, half]
    send(hid.at[:, other], h2.at[pl.ds(TOK, TOK)], mate_s.at[0], mate_r.at[0], mate)

    wait(encb.at[0:3, :, 0], enc_r.at[1])
    send(encb.at[:, :, c], encb.at[:, :, c], enc_s.at[2], enc_r.at[2], mate)
    wait(encb.at[:, :, 0], enc_r.at[2])
    weights = tap_w[...]
    weights = weights / jnp.sum(weights, axis=1, keepdims=True)
    rows = tap_rows[...]
    lane = lax.broadcasted_iota(jnp.int32, (TOK, 1536), 1)
    mix = sum(jnp.where(lane == rows[:, k : k + 1], weights[:, k : k + 1], 0.0) for k in range(4))
    target = dot(mix.astype(BF), encb[...].reshape(1536, 384), 1, 0)
    tgs[...] = target.astype(BF)

    def trows(tt):
        return pl.ds(pl.multiple_of(tt * 32, 32), 32)

    for d in (2, 1, 3):
        send(tgs.at[trows(up(t, d))], tgt.at[t], tg_s, tg_r, zpeer[d])
    tgt[t] = tgs[trows(t)]

    wait(irecv, i_r)
    total = inner[...] + irecv[0].astype(F32) + irecv[1].astype(F32) + irecv[2].astype(F32)
    inner[...] = total
    act[...] = (total / (1.0 + jnp.exp(-total))).astype(BF)
    a2[0:TOK] = act[:, half]
    send(act.at[:, other], a2.at[pl.ds(TOK, TOK)], mate_s.at[1], mate_r.at[1], mate)

    psend[...] = dot(act[...], wout[...], 1, 0).astype(BF)
    for d in (2, 1, 3):
        send(psend.at[trows(up(t, d))], precv.at[d - 1], p_s, p_r, zpeer[d])
    wait(tgt.at[0:3], tg_r)
    wait(precv, p_r)
    proj = psend[trows(t)].astype(F32)
    proj = proj + precv[0].astype(F32) + precv[1].astype(F32) + precv[2].astype(F32)
    tg = jnp.concatenate([tgt[s].astype(F32) for s in range(4)], axis=1)
    norm_p = jnp.sqrt(jnp.sum(proj * proj, axis=1, keepdims=True) + eps)
    norm_t = jnp.sqrt(jnp.sum(tg * tg, axis=1, keepdims=True) + eps)
    cosine = jnp.sum(proj * tg, axis=1, keepdims=True) / (norm_p * norm_t)
    factor = loss_scale / ALL_TOKENS
    g2[trows(t)] = (
        -factor * (tg / (norm_p * norm_t) - cosine * proj / (norm_p * norm_p))
    ).astype(BF)
    for d in (2, 1, 3):
        send(g2.at[trows(t)], g2.at[trows(t)], g_s, g_r, zpeer[d])
    wait(g2.at[0:96], g_r)
    send(g2.at[0:TOK], g2.at[pl.ds(TOK, TOK)], mate_s.at[2], mate_r.at[2], mate)

    grad_act = dot(g2[0:TOK], wout[...], 1, 1)
    v = inner[...]
    sig = 1.0 / (1.0 + jnp.exp(-v))
    gi2[t, 0:TOK] = (grad_act * (sig * (1.0 + v * (1.0 - sig)))).astype(BF)
    for d in (2, 1, 3):
        send(gi2.at[t, pl.ds(0, TOK)], gi2.at[t, pl.ds(0, TOK)], gi_s, gi_r.at[d - 1], zpeer[d])
    send(gi2.at[t, pl.ds(0, TOK)], gi2.at[t, pl.ds(TOK, TOK)], mg_s, mg_r.at[0], mate)

    def stage1_a(pa, ra, k):
        for d in (2, 1, 3):
            send(pa.at[up(y, d)], ra.at[d - 1], red_s.at[k], red_r.at[k], ypeer[d])

    def stage1_b(pb, rb, k):
        for d in (2, 1, 3):
            send(pb.at[:, up(x, d)], rb.at[d - 1], red_s.at[k + 1], red_r.at[k + 1], xpeer[d])

    def stage2(pa, pb, ra, rb, sa, sb, ta, tb, k):
        wait(ra, red_r.at[k])
        sa[...] = (pa[y].astype(F32) + sum(ra[i].astype(F32) for i in range(3))).astype(BF)
        for d in (2, 1, 3):
            send(sa.at[up(x, d)], ta.at[d - 1], red_s.at[k + 2], red_r.at[k + 2], xpeer[d])
        wait(rb, red_r.at[k + 1])
        sb[...] = (pb[:, x].astype(F32) + sum(rb[i].astype(F32) for i in range(3))).astype(BF)
        for d in (2, 1, 3):
            send(sb.at[up(y, d)], tb.at[d - 1], red_s.at[k + 3], red_r.at[k + 3], ypeer[d])

    def stage3(sa, sb, ta, tb, f, ex, k, own):
        wait(ta, red_r.at[k + 2])
        wait(tb, red_r.at[k + 3])
        f[:, 0:128] = (sa[x].astype(F32) + sum(ta[i].astype(F32) for i in range(3))).astype(BF)
        f[:, 128:256] = (sb[y].astype(F32) + sum(tb[i].astype(F32) for i in range(3))).astype(BF)
        mates = pl.ds(pl.multiple_of((1 - c) * own, 16), own)
        ours = pl.ds(pl.multiple_of(c * own, 16), own)
        send(f.at[mates], ex.at[2], red_s.at[k + 4], red_r.at[k + 4], at(y, x, 1 - c, dd=1 - dp))
        send(f.at[ours], ex.at[1], red_s.at[k + 4], red_r.at[k + 4], at(y, x, c, dd=1 - dp))
        send(f.at[mates], ex.at[0], red_s.at[k + 4], red_r.at[k + 4], mate)

    def finish(f, ex, k, own, out):
        wait(ex, red_r.at[k + 4])
        ours = pl.ds(pl.multiple_of(c * own, 16), own)
        here = f[ours].astype(F32) + ex[1].astype(F32)
        there = ex[0].astype(F32) + ex[2].astype(F32)
        out[0:256, :] = jnp.where(c == 0, here, there).T
        out[256:512, :] = jnp.where(c == 0, there, here).T

    for k in (0, 1, 2):
        wait(a2.at[0:TOK] if k < 2 else g2.at[0:TOK], mate_r.at[k])
    for yy in range(4):
        block = dot(g2[:, yy * 384 : (yy + 1) * 384], a2[...], 0, 0).astype(BF)
        p2a[yy] = block[:, 0:128].reshape(4, 96, 128)
        p2b[yy] = block[:, 128:256].reshape(4, 96, 128)
    stage1_a(p2a, r2a, 0)
    stage1_b(p2b, r2b, 0)

    def first(s, start):
        part = dot(gi2[s, 0:TOK], win[:, slab(s)], 1, 1)
        dacc[...] = part if start else dacc[...] + part

    def outer(s, d):
        wait(gi2.at[0, pl.ds(0, TOK)], mg_r.at[d])
        block = dot(gi2[s], h2[...], 0, 0).astype(BF)
        p1a[s] = block[:, 0:128].reshape(4, 128, 128)
        p1b[s] = block[:, 128:256].reshape(4, 128, 128)

    first(t, True)
    outer(t, 0)
    stage2(p2a, p2b, r2a, r2b, s2a, s2b, t2a, t2b, 0)
    for d in (1, 3, 2):
        s = up(t, 4 - d)
        wait(gi2.at[0, pl.ds(0, TOK)], gi_r.at[d - 1])
        send(gi2.at[s, pl.ds(0, TOK)], gi2.at[s, pl.ds(TOK, TOK)], mg_s, mg_r.at[d], mate)
        first(s, False)
        outer(s, d)
        if d == 1:
            stage3(s2a, s2b, t2a, t2b, f2, e2, 0, 48)
    stage1_a(p1a, r1a, 5)
    stage1_b(p1b, r1b, 5)
    d_out[...] = dacc[...].astype(BF)
    finish(f2, e2, 0, 48, gout_out)
    stage2(p1a, p1b, r1a, r1b, s1a, s1b, t1a, t1b, 5)
    stage3(s1a, s1b, t1a, t1b, f1, e1, 5, 64)

    for j in (0, 1):
        for n in (0, 1, 2):
            wait(qkv.at[j, n, pl.ds(0, 7)], qkv_s.at[j, n])
        wait(osend.at[j, pl.ds(0, 7)], o_s.at[j])
    wait(ssend.at[pl.ds(0, 7)], st_s)
    wait(encb.at[0, pl.ds(0, 3), 0], enc_s.at[0])
    wait(encb.at[0:3, :, 0], enc_s.at[1])
    wait(encb.at[:, :, 0], enc_s.at[2])
    wait(tgt.at[0:3], tg_s)
    wait(isend, i_s)
    wait(precv, p_s)
    wait(g2.at[0:96], g_s)
    wait(gi2.at[pl.ds(0, 3), pl.ds(0, TOK)], gi_s)
    wait(gi2.at[:, pl.ds(0, TOK)], mg_s)
    wait(a2.at[0:TOK], mate_s.at[0])
    wait(a2.at[0:TOK], mate_s.at[1])
    wait(g2.at[0:TOK], mate_s.at[2])
    for k, ra, rb, ta, tb, ex in ((0, r2a, r2b, t2a, t2b, e2), (5, r1a, r1b, t1a, t1b, e1)):
        wait(ra, red_s.at[k])
        wait(rb, red_s.at[k + 1])
        wait(ta, red_s.at[k + 2])
        wait(tb, red_s.at[k + 3])
        wait(ex, red_s.at[k + 4])
    finish(f1, e1, 5, 64, gin_out)


def grad_scratch(rows):
    return [
        VMEM((4, 4, rows, 128), BF),
        VMEM((4, 4, rows, 128), BF),
        VMEM((3, 4, rows, 128), BF),
        VMEM((3, 4, rows, 128), BF),
        VMEM((4, rows, 128), BF),
        VMEM((4, rows, 128), BF),
        VMEM((3, rows, 128), BF),
        VMEM((3, rows, 128), BF),
        VMEM((rows, 256), BF),
        VMEM((3, rows // 2, 256), BF),
    ]


def local(
    residual, queries, attn_keys, attn_values, gate_table, timesteps, enc_feats,
    tap_rows, tap_weights, proj_in, proj_out,
):
    dma = pltpu.SemaphoreType.DMA
    vm = pl.BlockSpec(memory_space=VMEM)
    hb = pl.BlockSpec(memory_space=pl.ANY)
    sm = pl.BlockSpec(memory_space=pltpu.SMEM)
    d_hidden, gin, gout = pl.pallas_call(
        kernel,
        name="alignment",
        out_shape=(
            jax.ShapeDtypeStruct((TOK, 512), BF),
            jax.ShapeDtypeStruct((512, 64), F32),
            jax.ShapeDtypeStruct((512, 48), F32),
        ),
        in_specs=[vm, hb, hb, hb, hb, sm, hb, vm, vm, hb, hb],
        out_specs=(vm, vm, vm),
        scratch_shapes=[
            VMEM((2, 3, 8, TOK, HD), BF),
            VMEM((1000, 512), BF),
            VMEM((512, 2048), BF),
            VMEM((512, 1536), BF),
            VMEM((4, 4, 2, 48, 384), BF),
            VMEM((2, 8, HD, TOK), BF),
            VMEM((8, 2, 8, TOK), F32),
            VMEM((4, 2, 2, HD, TOK), BF),
            VMEM((4, 2, 2, 8, TOK), F32),
            VMEM((TOK, 384), BF),
            VMEM((4, 32, 384), BF),
            VMEM((TOK, 512), BF),
            VMEM((2 * TOK, 256), BF),
            VMEM((3, TOK, 512), BF),
            VMEM((3, TOK, 512), BF),
            VMEM((TOK, 512), F32),
            VMEM((TOK, 512), BF),
            VMEM((2 * TOK, 256), BF),
            VMEM((TOK, 1536), BF),
            VMEM((3, 32, 1536), BF),
            VMEM((2 * TOK, 1536), BF),
            VMEM((4, 2 * TOK, 512), BF),
            VMEM((TOK, 512), F32),
            *grad_scratch(128),
            *grad_scratch(96),
            dma((4,)),
            dma((2, 3)),
            dma((2, 3)),
            dma((3,)),
            dma((3,)),
            dma((2,)),
            dma((2,)),
            dma,
            dma,
            dma,
            dma,
            dma((3,)),
            dma((3,)),
            dma,
            dma,
            dma,
            dma,
            dma,
            dma,
            dma,
            dma((3,)),
            dma,
            dma((4,)),
            dma((10,)),
            dma((10,)),
        ],
        compiler_params=pltpu.CompilerParams(
            collective_id=0, has_side_effects=True, vmem_limit_bytes=56 << 20
        ),
        cost_estimate=pl.CostEstimate(
            flops=2_500_000_000, bytes_accessed=16_000_000, transcendentals=2_200_000
        ),
    )(
        residual[0], queries[0], attn_keys[0], attn_values[0], gate_table, timesteps,
        enc_feats[0], tap_rows[0], tap_weights[0], proj_in, proj_out,
    )
    return d_hidden[None], gin, gout


def solution(mesh):
    in_specs = (
        P("dp", "ctx", "tp"),
        P("dp", "ctx", "tp"),
        P("dp", "ctx", "tp"),
        P("dp", "ctx", "tp"),
        P(None, "tp"),
        P("dp"),
        P("dp", "ctx", "tp"),
        P("dp", "ctx", None),
        P("dp", "ctx", None),
        P("tp", None),
        P("tp", None),
    )
    out_specs = (P("dp", "ctx", "tp"), P("tp", "ctx"), P("tp", "ctx"))
    return jax.shard_map(local, mesh=mesh, in_specs=in_specs, out_specs=out_specs, check_vma=False)
```

```python
import functools
import math

import jax
import jax.numpy as jnp
from jax import lax
from jax.experimental import pallas as pl
from jax.experimental.pallas import tpu as pltpu
from jax.sharding import PartitionSpec as P

HD = 128
TOK = 128
eps = 1e-06
loss_scale = 4194304.0
ALL_TOKENS = 8192
BF = jnp.bfloat16
F32 = jnp.float32
MESH = pl.DeviceIdType.MESH
VMEM = pltpu.VMEM


def dot(a, b, ca, cb):
    return lax.dot_general(a, b, (((ca,), (cb,)), ((), ())), preferred_element_type=F32)


def kernel(
    res, q_in, k_in, v_in, gate_in, step, enc, tap_rows, tap_w, win_in, wout_in,
    d_out, gin_out, gout_out,
    qkv, gate, win, wcol, wout, encb, osend, orecv,
    tgs, tgt, hidf, inner, act, a2, psend, precv, g2, gi, gia, dacc,
    p1a, p1b, r1a, r1b, s1a, s1b, t1a, t1b, f1, e1,
    p2a, p2b, r2a, r2b, s2a, s2b, t2a, t2b, f2, e2,
    load_sem, qkv_s, qkv_r, w_s, w_r, enc_s, enc_r, o_s, o_r, tg_s, tg_r,
    mate_s, mate_r, hid_s, hid_r, p_s, p_r, g_s, g_r, gi_s, gi_r, red_s, red_r,
):
    ctx = lax.axis_index("ctx")
    t = lax.axis_index("tp")
    dp = lax.axis_index("dp")
    c = lax.rem(ctx, 2)
    x = lax.rem(lax.div(ctx, 2), 4)
    y = lax.div(ctx, 8)
    me = x * 2 + c
    mine = y * 2 + c

    def at(yy, xx, cc, tt=None, dd=None):
        return {
            "ctx": (yy * 4 + xx) * 2 + cc,
            "tp": t if tt is None else tt,
            "dp": dp if dd is None else dd,
        }

    def up(v, d):
        return lax.rem(v + d, 4)

    mate = at(y, x, 1 - c)
    zpeer = {d: at(y, x, c, tt=up(t, d)) for d in (1, 2, 3)}
    xpeer = {d: at(y, up(x, d), c) for d in (1, 2, 3)}
    ypeer = {d: at(up(y, d), x, c) for d in (1, 2, 3)}

    def send(src, dst, ss, rs, dev):
        cp = pltpu.make_async_remote_copy(
            src_ref=src, dst_ref=dst, send_sem=ss, recv_sem=rs, device_id=dev, device_id_type=MESH
        )
        cp.start()

    def wait(ref, sem):
        pltpu.make_async_copy(ref, ref, sem).wait()

    def cols(cc, j):
        return pl.ds(pl.multiple_of(cc * 256 + j * 128, 128), 128)

    half = pl.ds(pl.multiple_of(c * 256, 256), 256)
    other = pl.ds(pl.multiple_of((1 - c) * 256, 256), 256)

    def slab(tt):
        return pl.ds(pl.multiple_of(tt * 512, 512), 512)

    def trows(h, tt):
        return pl.ds(pl.multiple_of(h * 64 + tt * 16, 16), 16)

    for j in (0, 1):
        for n, src, slot in ((1, k_in, mine), (0, q_in, me), (2, v_in, mine)):
            pltpu.make_async_copy(src.at[:, cols(c, j)], qkv.at[j, n, slot], qkv_r.at[j, n]).start()
    pltpu.make_async_copy(enc, encb.at[y, x, c], load_sem.at[3]).start()
    for cc in (0, 1):
        pltpu.make_async_copy(
            win_in.at[pl.ds(2 * cc, 2), :, slab(t)], wcol.at[t, :, cc], load_sem.at[4]
        ).start()
    loads = [
        pltpu.make_async_copy(gate_in, gate, load_sem.at[2]),
        pltpu.make_async_copy(win_in, win, load_sem.at[0]),
        pltpu.make_async_copy(wout_in, wout, load_sem.at[1]),
    ]
    for cp in loads:
        cp.start()

    bar = pltpu.get_barrier_semaphore()
    partners = [at(y, up(x, d), cc) for d in (1, 2, 3) for cc in (0, 1)]
    partners += [at(up(y, d), x, cc) for d in (1, 2, 3) for cc in (0, 1)]
    partners += [mate, at(y, x, c, dd=1 - dp)]
    near = up(t, 3 - 2 * dp)
    far = up(t, 2)
    partners += [at(y, x, c, tt=near, dd=1 - dp), at(y, x, c, tt=far, dd=1 - dp)]
    partners += [zpeer[d] for d in (2, 1, 3)]
    owner = (t, 2 * c + lax.div(x, 2), lax.rem(x, 2), up(y, t))
    giver = (up(t, 4 - y), 2 * lax.rem(x, 2) + c, lax.div(x, 2), y)
    keeps = jnp.logical_and(
        jnp.logical_and(owner[0] == y, owner[1] == x), jnp.logical_and(owner[2] == c, owner[3] == t)
    )
    for p in reversed(partners):
        pl.semaphore_signal(bar, inc=1, device_id=p, device_id_type=MESH)
    pl.semaphore_signal(
        bar, inc=1, device_id=at(*giver, dd=1 - dp), device_id_type=MESH
    )

    @pl.when(jnp.logical_not(keeps))
    def _():
        pl.semaphore_signal(bar, inc=1, device_id=at(*giver), device_id_type=MESH)

    pl.semaphore_wait(bar, len(partners) + 2 - keeps.astype(jnp.int32))

    for j in (0, 1):
        for n, src, axis in ((1, k_in, 0), (0, q_in, 1), (2, v_in, 0)):
            ss, rs = qkv_s.at[j, n], qkv_r.at[j, n]
            slot = me if axis == 1 else mine
            for d in (2, 1, 3, 0):
                for e in (0, 1):
                    if d == 0 and e == 0:
                        continue
                    cc = lax.rem(c + e, 2)
                    dev = at(y, up(x, d), cc) if axis == 1 else at(up(y, d), x, cc)
                    send(src.at[:, cols(cc, j)], qkv.at[j, n, slot], ss, rs, dev)
        if j == 0:
            for d in (1, 2, 3):
                send(enc, encb.at[y, x, c], enc_s.at[0], enc_r.at[0], xpeer[d])

    send(win_in.at[pl.ds(2 * c, 2), :, slab(near)], wcol.at[t, :, c], w_s.at[0], w_r.at[0],
         at(y, x, c, tt=near, dd=1 - dp))
    send(win_in.at[2 * c + 1 - dp, :, slab(far)], wcol.at[t, 1 - dp, c], w_s.at[1], w_r.at[1],
         at(y, x, c, tt=far, dd=1 - dp))

    for cp in loads:
        cp.wait()
    pick = (lax.broadcasted_iota(jnp.int32, (16, gate.shape[0]), 1) == step[0]).astype(F32).astype(BF)
    gate_row = dot(pick, gate[...], 1, 0)[0:1]
    base = res[...].astype(F32)

    scale = HD ** (-0.5) * math.log2(math.e)

    def keys_of(j):
        for n in (1, 0, 2):
            wait(qkv.at[j, n], qkv_r.at[j, n])
        return qkv[j, 1].reshape(8 * TOK, HD), qkv[j, 2].reshape(8 * TOK, HD).T

    def block(j, h, it, keys, vt):
        xs = (up(x, 1 + 2 * it), up(x, 2 + 2 * it))
        slots = [2 * xq + cc for xq in xs for cc in (0, 1)]
        rows = pl.ds(pl.multiple_of(h * 64, 64), 64)
        qb = jnp.concatenate([qkv[j, 0, s, rows] for s in slots], axis=0)
        st = dot(keys, qb, 1, 1) * scale
        top = jnp.max(st, axis=0, keepdims=True)
        expo = jnp.exp2(st - top)
        total = jnp.sum(expo, axis=0, keepdims=True)
        out = (dot(vt, expo.astype(BF), 1, 0) / total).T.astype(BF)
        lse = top + jnp.log2(total)
        high = lse.astype(BF).astype(F32)
        mid = (lse - high).astype(BF).astype(F32)
        line = lax.broadcasted_iota(jnp.int32, (16, 256), 0)
        lses = jnp.where(line == 0, high, jnp.where(line == 1, mid, lse - high - mid)).astype(BF)
        for k, slot in enumerate(slots):
            xq, cc = xs[k // 2], k % 2
            osend[j, h, slot, 0:64] = out[64 * k : 64 * k + 64]
            osend[j, h, slot, 64:80] = lses[:, 128 * (k // 2) : 128 * (k // 2) + 128]
            own = jnp.logical_and(xq == x, cc == c)

            @pl.when(own)
            def _():
                pltpu.make_async_copy(osend.at[j, h, slot], orecv.at[h, x, c, j], o_r.at[j, h]).start()

            @pl.when(jnp.logical_not(own))
            def _():
                send(osend.at[j, h, slot], orecv.at[h, x, c, j], o_s.at[j, h], o_r.at[j, h], at(y, xq, cc))

    def combine(j, h):
        wait(orecv.at[h, :, :, j], o_r.at[j, h])
        lses = [
            jnp.concatenate(
                [
                    jnp.sum(orecv[h, i, cc, j, 64:80].astype(F32)[0:3], axis=0, keepdims=True)
                    for cc in (0, 1)
                ],
                axis=0,
            )
            for i in range(4)
        ]
        top = jnp.maximum(jnp.maximum(lses[0], lses[1]), jnp.maximum(lses[2], lses[3]))
        ws = [jnp.exp2(v - top) for v in lses]
        inv = 1.0 / (ws[0] + ws[1] + ws[2] + ws[3])
        wt = jnp.concatenate([w * inv for w in ws], axis=0).T
        wt = jnp.where(c == 0, wt[0:64], wt[64:128])
        r = 64 * h
        for cc in (0, 1):
            acc = sum(
                orecv[h, i, cc, j, 0:64].astype(F32) * wt[:, 2 * i + cc : 2 * i + cc + 1] for i in range(4)
            )
            lo = (2 * cc + j) * HD
            hidf[t, j, r : r + 64, cc * HD : cc * HD + HD] = (
                base[r : r + 64, lo : lo + HD] + gate_row[:, lo : lo + HD] * acc
            ).astype(BF)

    def share(j, rows, k):
        for d in (2, 1, 3):
            send(hidf.at[t, j, rows], hidf.at[t, j, rows], hid_s.at[k], hid_r.at[k], zpeer[d])

    keys, vt = keys_of(0)
    for h in (0, 1):

        def loop0(it, carry):
            block(0, h, it, keys, vt)
            return carry

        lax.fori_loop(0, 2, loop0, 0)
        pair = at(y, x, c, dd=1 - dp)
        if h == 0:
            wait(wcol.at[0, :, 0], w_r.at[0])
            send(wcol.at[near, :, c], wcol.at[near, :, c], w_s.at[2], w_r.at[2], pair)
        else:
            wait(wcol.at[0, 0, 0], w_r.at[1])
            send(wcol.at[far, dp, c], wcol.at[far, dp, c], w_s.at[3], w_r.at[3], pair)

    wait(enc, load_sem.at[3])
    wait(encb.at[0, pl.ds(0, 3), 0], enc_r.at[0])
    for d in (2, 1, 3):
        send(encb.at[y, :, c], encb.at[y, :, c], enc_s.at[1], enc_r.at[1], ypeer[d])

    keys1, vt1 = keys_of(1)
    for h in (0, 1):

        def loop1(it, carry):
            block(1, h, it, keys1, vt1)
            return carry

        lax.fori_loop(0, 2, loop1, 0)
        if h == 0:
            combine(0, 0)
            combine(0, 1)
            share(0, pl.ds(0, TOK), 0)
    combine(1, 0)
    share(1, pl.ds(0, 64), 1)

    wait(wcol.at[0, :, 0], w_r.at[2])
    wait(wcol.at[0, 0, 0], w_r.at[3])
    for d in (1, 2, 3):
        s = up(t, d)
        send(wcol.at[s, :, c], wcol.at[s, :, c], w_s.at[4], w_r.at[4], mate)
    wait(encb.at[0:3, :, 0], enc_r.at[1])
    send(encb.at[:, :, c], encb.at[:, :, c], enc_s.at[2], enc_r.at[2], mate)
    combine(1, 1)
    share(1, pl.ds(64, 64), 2)

    def first_end(h):
        rows = pl.ds(64 * h, 64)
        wait(hidf.at[pl.ds(0, 3), 1, pl.ds(0, 64)], hid_r.at[1 + h])
        total = inner[rows] + sum(
            dot(hidf[s, 1, rows], wcol[s, 1].reshape(256, 512), 1, 0) for s in range(4)
        )
        inner[rows] = total
        act[rows] = (total / (1.0 + jnp.exp(-total))).astype(BF)

    def last_start(h):
        rows = pl.ds(64 * h, 64)
        psend[rows] = dot(act[rows], wout[...], 1, 0).astype(BF)
        for d in (2, 1, 3):
            send(psend.at[trows(h, up(t, d))], precv.at[h, d - 1], p_s.at[h], p_r.at[h], zpeer[d])

    def loss(h):
        wait(tgt.at[h, pl.ds(0, 3)], tg_r.at[h])
        tg = jnp.concatenate([tgt[h, s].astype(F32) for s in range(4)], axis=1)
        norm_t = jnp.sqrt(jnp.sum(tg * tg, axis=1, keepdims=True) + eps)
        wait(precv.at[h], p_r.at[h])
        proj = psend[trows(h, t)].astype(F32) + sum(precv[h, i].astype(F32) for i in range(3))
        norm_p = jnp.sqrt(jnp.sum(proj * proj, axis=1, keepdims=True) + eps)
        cosine = jnp.sum(proj * tg, axis=1, keepdims=True) / (norm_p * norm_t)
        factor = loss_scale / ALL_TOKENS
        own = trows(h, t)
        g2[own] = (-factor * (tg / (norm_p * norm_t) - cosine * proj / (norm_p * norm_p))).astype(BF)
        for d in (2, 1, 3):
            send(g2.at[own], g2.at[own], g_s.at[h], g_r.at[h], zpeer[d])

    def hidden_grad(h):
        rows = pl.ds(64 * h, 64)
        mrows = pl.ds(TOK + 64 * h, 64)
        wait(g2.at[0:48], g_r.at[h])
        send(g2.at[rows], g2.at[mrows], mate_s.at[2 + h], mate_r.at[2 + h], mate)
        v = inner[rows]
        sig = 1.0 / (1.0 + jnp.exp(-v))
        grad_act = dot(g2[rows], wout[...], 1, 1)
        gi[t, rows] = (grad_act * (sig * (1.0 + v * (1.0 - sig)))).astype(BF)
        for d in (2, 1, 3):
            send(gi.at[t, rows], gi.at[t, rows], gi_s, gi_r.at[d - 1], zpeer[d])
        send(gi.at[t, rows, other], gia.at[mrows], mate_s.at[4 + h], mate_r.at[4 + h], mate)

    weights = tap_w[...]
    weights = weights / jnp.sum(weights, axis=0, keepdims=True)
    taps = jnp.concatenate([tap_rows[...].astype(F32), weights], axis=0).T
    rows, weights = taps[:, 0:4], taps[:, 4:8]
    lane = lax.broadcasted_iota(jnp.int32, (TOK, 1536), 1).astype(F32)
    mix = sum(jnp.where(lane == rows[:, k : k + 1], weights[:, k : k + 1], 0.0) for k in range(4))
    wait(encb.at[:, :, 0], enc_r.at[2])
    tgs[...] = dot(mix.astype(BF), encb[...].reshape(1536, 384), 1, 0).astype(BF)
    for h in (0, 1):
        for d in (2, 1, 3):
            send(tgs.at[trows(h, up(t, d))], tgt.at[h, t], tg_s.at[h], tg_r.at[h], zpeer[d])
        tgt[h, t] = tgs[trows(h, t)]

    wait(wcol.at[0], load_sem.at[4])
    wait(wcol.at[pl.ds(0, 3), :, 0], w_r.at[4])
    wait(hidf.at[pl.ds(0, 3), 0, pl.ds(0, TOK)], hid_r.at[0])
    inner[...] = sum(dot(hidf[s, 0, 0:TOK], wcol[s, 0].reshape(256, 512), 1, 0) for s in range(4))
    for h in (0, 1):
        first_end(h)
        last_start(h)
    send(hidf.at[:, :, pl.ds(0, TOK)], hidf.at[:, :, pl.ds(TOK, TOK)], mate_s.at[0], mate_r.at[0], mate)
    a2[0:TOK] = act[:, half]
    send(act.at[:, other], a2.at[pl.ds(TOK, TOK)], mate_s.at[1], mate_r.at[1], mate)
    for h in (0, 1):
        loss(h)
    for h in (0, 1):
        hidden_grad(h)

    wait(a2.at[0:TOK], mate_r.at[1])
    for h in (0, 1):
        wait(g2.at[0:64], mate_r.at[2 + h])
    for yy in range(4):
        part = dot(g2[:, yy * 384 : (yy + 1) * 384], a2[...], 0, 0).astype(BF)
        p2a[yy] = part[:, 0:128].reshape(4, 96, 128)
        p2b[yy] = part[:, 128:256].reshape(4, 96, 128)
    gia[0:TOK] = gi[t, :, half]
    wait(hidf.at[:, :, pl.ds(0, TOK)], mate_r.at[0])
    for h in (0, 1):
        wait(gia.at[0:64], mate_r.at[4 + h])
    for d in (2, 1, 3, 0):
        s = up(up(y, d), t)
        p1a[s] = dot(gia[...], hidf[s, 0], 0, 0).astype(BF)
        p1b[:, s] = dot(gia[...], hidf[s, 1], 0, 0).astype(BF).reshape(4, 64, 256)
        if d:
            send(p1a.at[s], r1a.at[d - 1], red_s.at[0], red_r.at[0], ypeer[d])
    for d in (2, 1, 3):
        send(p1b.at[up(x, d)], r1b.at[d - 1], red_s.at[1], red_r.at[1], xpeer[d])
    for d in (2, 1, 3):
        send(p2a.at[up(y, d)], r2a.at[d - 1], red_s.at[5], red_r.at[5], ypeer[d])
        send(p2b.at[:, up(x, d)], r2b.at[d - 1], red_s.at[6], red_r.at[6], xpeer[d])

    def first(s, start):
        part = dot(gi[s], win[:, :, slab(s)].reshape(512, 512), 1, 1)
        dacc[...] = part if start else dacc[...] + part

    first(t, True)

    block_mine = up(y, t)
    wait(r1a, red_r.at[0])
    total = p1a[block_mine].astype(F32) + sum(r1a[i].astype(F32) for i in range(3))
    s1a[...] = total.astype(BF).reshape(4, 64, 256)
    for d in (2, 1, 3):
        send(s1a.at[up(x, d)], t1a.at[d - 1], red_s.at[2], red_r.at[2], xpeer[d])
    wait(r1b, red_r.at[1])
    s1b[...] = (p1b[x].astype(F32) + sum(r1b[i].astype(F32) for i in range(3))).astype(BF)
    for d in (2, 1, 3):
        send(s1b.at[up(up(y, d), t)], t1b.at[d - 1], red_s.at[3], red_r.at[3], ypeer[d])

    wait(r2a, red_r.at[5])
    s2a[...] = (p2a[y].astype(F32) + sum(r2a[i].astype(F32) for i in range(3))).astype(BF)
    wait(r2b, red_r.at[6])
    s2b[...] = (p2b[:, x].astype(F32) + sum(r2b[i].astype(F32) for i in range(3))).astype(BF)
    for d in (2, 1, 3, 0):
        for e in (0, 1):
            cc = lax.rem(c + e, 2)
            part = pl.ds(pl.multiple_of(cc * 48, 16), 48)
            xq, yq = up(x, d), up(y, d)
            if d == 0 and e == 0:
                pltpu.make_async_copy(s2a.at[x, part], t2a.at[c, x], red_r.at[7]).start()
                pltpu.make_async_copy(s2b.at[y, part], t2b.at[c, y], red_r.at[8]).start()
            else:
                k = 7 if d else 8
                send(s2a.at[xq, part], t2a.at[c, x], red_s.at[k], red_r.at[7], at(y, xq, cc))
                send(s2b.at[yq, part], t2b.at[c, y], red_s.at[k], red_r.at[8], at(yq, x, cc))

    wait(t1a, red_r.at[2])
    f1[0] = (s1a[x].astype(F32) + sum(t1a[i].astype(F32) for i in range(3))).astype(BF)
    wait(t1b, red_r.at[3])
    f1[1] = (s1b[block_mine].astype(F32) + sum(t1b[i].astype(F32) for i in range(3))).astype(BF)
    send(f1, e1.at[dp], red_s.at[4], red_r.at[4], at(*owner, dd=1 - dp))

    @pl.when(keeps)
    def _():
        pltpu.make_async_copy(f1, e1.at[dp], red_r.at[4]).start()

    @pl.when(jnp.logical_not(keeps))
    def _():
        send(f1, e1.at[dp], red_s.at[4], red_r.at[4], at(*owner))

    wait(t2a, red_r.at[7])
    wait(t2b, red_r.at[8])
    for cc in (0, 1):
        for n, f in enumerate((t2a, t2b)):
            total = sum(f[cc, i].astype(F32) for i in range(4))
            f2[:, 256 * cc + 128 * n : 256 * cc + 128 * n + 128] = total.astype(BF)
    send(f2, e2, red_s.at[9], red_r.at[9], pair)

    for d in (1, 3, 2):
        s = up(t, 4 - d)
        wait(gi.at[0], gi_r.at[d - 1])
        first(s, False)
    d_out[...] = dacc[...].astype(BF)

    for j in (0, 1):
        for n in (0, 1, 2):
            wait(qkv.at[j, n, pl.ds(0, 7)], qkv_s.at[j, n])
        for h in (0, 1):
            wait(osend.at[j, h, pl.ds(0, 7)], o_s.at[j, h])
    wait(wcol.at[0, :, 0], w_s.at[0])
    wait(wcol.at[0, 0, 0], w_s.at[1])
    wait(wcol.at[0, :, 0], w_s.at[2])
    wait(wcol.at[0, 0, 0], w_s.at[3])
    wait(wcol.at[pl.ds(0, 3), :, 0], w_s.at[4])
    wait(encb.at[0, pl.ds(0, 3), 0], enc_s.at[0])
    wait(encb.at[0:3, :, 0], enc_s.at[1])
    wait(encb.at[:, :, 0], enc_s.at[2])
    wait(hidf.at[pl.ds(0, 3), 0, pl.ds(0, TOK)], hid_s.at[0])
    wait(hidf.at[:, :, pl.ds(0, TOK)], mate_s.at[0])
    wait(a2.at[0:TOK], mate_s.at[1])
    for h in (0, 1):
        wait(hidf.at[pl.ds(0, 3), 1, pl.ds(0, 64)], hid_s.at[1 + h])
        wait(tgt.at[h, pl.ds(0, 3)], tg_s.at[h])
        wait(precv.at[h], p_s.at[h])
        wait(g2.at[0:48], g_s.at[h])
        wait(g2.at[0:64], mate_s.at[2 + h])
        wait(gia.at[0:64], mate_s.at[4 + h])
    wait(gi.at[pl.ds(0, 3)], gi_s)
    wait(r1a, red_s.at[0])
    wait(r1b, red_s.at[1])
    wait(t1a, red_s.at[2])
    wait(t1b, red_s.at[3])
    wait(r2a, red_s.at[5])
    wait(r2b, red_s.at[6])
    wait(r2a.at[:, pl.ds(0, 2)], red_s.at[7])
    wait(s2a.at[0], red_s.at[8])
    wait(f2, red_s.at[9])

    @pl.when(keeps)
    def _():
        wait(f1, red_s.at[4])

    @pl.when(jnp.logical_not(keeps))
    def _():
        wait(e1, red_s.at[4])

    wait(e2, red_r.at[9])
    gout_out[...] = f2[...].astype(F32) + e2[...].astype(F32)
    wait(e1, red_r.at[4])
    for j in (0, 1):
        total = e1[0, j].astype(F32) + e1[1, j].astype(F32)
        for cc in (0, 1):
            lo = (2 * cc + j) * HD
            gin_out[:, lo : lo + HD] = total[:, cc * HD : cc * HD + HD]


def keep(a, b, c, a_out, b_out, c_out):
    a_out[...] = a[...]
    b_out[...] = b[...]
    c_out[...] = c[...]


def local(
    residual, queries, attn_keys, attn_values, gate_table, timesteps, enc_feats,
    tap_rows, tap_weights, proj_in, proj_out,
):
    dma = pltpu.SemaphoreType.DMA
    vm = pl.BlockSpec(memory_space=VMEM)
    hb = pl.BlockSpec(memory_space=pl.ANY)
    sm = pl.BlockSpec(memory_space=pltpu.SMEM)
    d_hidden, gin, gout = pl.pallas_call(
        kernel,
        name="alignment",
        out_shape=(
            jax.ShapeDtypeStruct((TOK, 512), BF),
            jax.ShapeDtypeStruct((64, 512), F32),
            jax.ShapeDtypeStruct((48, 512), F32),
        ),
        in_specs=[vm, hb, hb, hb, hb, sm, hb, vm, vm, hb, hb],
        out_specs=(vm, vm, vm),
        scratch_shapes=[
            VMEM((2, 3, 8, TOK, HD), BF),
            VMEM((1000, 512), BF),
            VMEM((4, HD, 2048), BF),
            VMEM((4, 2, 2, HD, 512), BF),
            VMEM((512, 1536), BF),
            VMEM((4, 4, 2, 48, 384), BF),
            VMEM((2, 2, 8, 80, HD), BF),
            VMEM((2, 4, 2, 2, 80, HD), BF),
            VMEM((TOK, 384), BF),
            VMEM((2, 4, 16, 384), BF),
            VMEM((4, 2, 2 * TOK, 256), BF),
            VMEM((TOK, 512), F32),
            VMEM((TOK, 512), BF),
            VMEM((2 * TOK, 256), BF),
            VMEM((TOK, 1536), BF),
            VMEM((2, 3, 16, 1536), BF),
            VMEM((2 * TOK, 1536), BF),
            VMEM((4, TOK, 512), BF),
            VMEM((2 * TOK, 256), BF),
            VMEM((TOK, 512), F32),
            VMEM((4, 256, 256), BF),
            VMEM((4, 4, 64, 256), BF),
            VMEM((3, 256, 256), BF),
            VMEM((3, 4, 64, 256), BF),
            VMEM((4, 64, 256), BF),
            VMEM((4, 64, 256), BF),
            VMEM((3, 64, 256), BF),
            VMEM((3, 64, 256), BF),
            VMEM((2, 64, 256), BF),
            VMEM((2, 2, 64, 256), BF),
            VMEM((4, 4, 96, 128), BF),
            VMEM((4, 4, 96, 128), BF),
            VMEM((3, 4, 96, 128), BF),
            VMEM((3, 4, 96, 128), BF),
            VMEM((4, 96, 128), BF),
            VMEM((4, 96, 128), BF),
            VMEM((2, 4, 48, 128), BF),
            VMEM((2, 4, 48, 128), BF),
            VMEM((48, 512), BF),
            VMEM((48, 512), BF),
            dma((5,)),
            dma((2, 3)),
            dma((2, 3)),
            dma((5,)),
            dma((5,)),
            dma((3,)),
            dma((3,)),
            dma((2, 2)),
            dma((2, 2)),
            dma((2,)),
            dma((2,)),
            dma((6,)),
            dma((6,)),
            dma((3,)),
            dma((3,)),
            dma((2,)),
            dma((2,)),
            dma((2,)),
            dma((2,)),
            dma,
            dma((3,)),
            dma((10,)),
            dma((10,)),
        ],
        compiler_params=pltpu.CompilerParams(
            collective_id=0, has_side_effects=True, vmem_limit_bytes=56 << 20
        ),
        cost_estimate=pl.CostEstimate(
            flops=2_500_000_000, bytes_accessed=16_000_000, transcendentals=2_200_000
        ),
    )(
        residual[0], queries[0], attn_keys[0], attn_values[0], gate_table, timesteps,
        enc_feats[0], tap_rows[0].T, tap_weights[0].T, proj_in.reshape(4, HD, 2048), proj_out,
    )
    d_hidden, gin, gout = pl.pallas_call(
        keep,
        name="keep",
        out_shape=(
            jax.ShapeDtypeStruct((TOK, 512), BF),
            jax.ShapeDtypeStruct((64, 512), F32),
            jax.ShapeDtypeStruct((48, 512), F32),
        ),
        in_specs=[vm, vm, vm],
        out_specs=(vm, vm, vm),
    )(d_hidden, gin, gout)
    return d_hidden[None], gin.T, gout.T


def solution(mesh):
    in_specs = (
        P("dp", "ctx", "tp"),
        P("dp", "ctx", "tp"),
        P("dp", "ctx", "tp"),
        P("dp", "ctx", "tp"),
        P(None, "tp"),
        P("dp"),
        P("dp", "ctx", "tp"),
        P("dp", "ctx", None),
        P("dp", "ctx", None),
        P("tp", None),
        P("tp", None),
    )
    out_specs = (P("dp", "ctx", "tp"), P("tp", "ctx"), P("tp", "ctx"))
    return jax.shard_map(local, mesh=mesh, in_specs=in_specs, out_specs=out_specs, check_vma=False)
```

```python
import functools
import math

import jax
import jax.numpy as jnp
from jax import lax
from jax.experimental import pallas as pl
from jax.experimental.pallas import tpu as pltpu
from jax.sharding import PartitionSpec as P

HD = 128
TOK = 128
eps = 1e-06
loss_scale = 4194304.0
ALL_TOKENS = 8192
BF = jnp.bfloat16
F32 = jnp.float32
MESH = pl.DeviceIdType.MESH
VMEM = pltpu.VMEM


def dot(a, b, ca, cb):
    return lax.dot_general(a, b, (((ca,), (cb,)), ((), ())), preferred_element_type=F32)


def kernel(
    res, q_in, k_in, v_in, gate_in, step, enc, tap_rows, tap_w, win_in, wout_in,
    d_out, gin_out, gout_out,
    qkv, gate, win, wcol, wout, encb, osend, orecv,
    scores, tops, tgs, tgt, hidf, inner, act, a2, psend, precv, g2, gi, gia, dacc,
    p1a, p1b, r1a, r1b, s1a, s1b, t1a, t1b, f1, e1,
    p2a, p2b, r2a, r2b, s2a, s2b, t2a, t2b, f2, e2,
    load_sem, qkv_s, qkv_r, kv_s, kv_r, w_s, w_r, enc_s, enc_r, o_s, o_r, tg_s, tg_r,
    mate_s, mate_r, hid_s, hid_r, p_s, p_r, g_s, g_r, gi_s, gi_r, red_s, red_r,
):
    ctx = lax.axis_index("ctx")
    t = lax.axis_index("tp")
    dp = lax.axis_index("dp")
    c = lax.rem(ctx, 2)
    x = lax.rem(lax.div(ctx, 2), 4)
    y = lax.div(ctx, 8)
    me = x * 2 + c
    mine = y * 2 + c

    def at(yy, xx, cc, tt=None, dd=None):
        return {
            "ctx": (yy * 4 + xx) * 2 + cc,
            "tp": t if tt is None else tt,
            "dp": dp if dd is None else dd,
        }

    def up(v, d):
        return lax.rem(v + d, 4)

    mate = at(y, x, 1 - c)
    zpeer = {d: at(y, x, c, tt=up(t, d)) for d in (1, 2, 3)}
    xpeer = {d: at(y, up(x, d), c) for d in (1, 2, 3)}
    ypeer = {d: at(up(y, d), x, c) for d in (1, 2, 3)}

    def send(src, dst, ss, rs, dev):
        cp = pltpu.make_async_remote_copy(
            src_ref=src, dst_ref=dst, send_sem=ss, recv_sem=rs, device_id=dev, device_id_type=MESH
        )
        cp.start()

    def wait(ref, sem):
        pltpu.make_async_copy(ref, ref, sem).wait()

    def cols(cc, j):
        return pl.ds(pl.multiple_of(cc * 256 + j * 128, 128), 128)

    half = pl.ds(pl.multiple_of(c * 256, 256), 256)
    other = pl.ds(pl.multiple_of((1 - c) * 256, 256), 256)

    def slab(tt):
        return pl.ds(pl.multiple_of(tt * 512, 512), 512)

    def trows(h, tt):
        return pl.ds(pl.multiple_of(h * 64 + tt * 16, 16), 16)

    for j in (0, 1):
        for n, src, slot in ((1, k_in, mine), (0, q_in, me), (2, v_in, mine)):
            pltpu.make_async_copy(src.at[:, cols(c, j)], qkv.at[j, n, slot], qkv_r.at[j, n]).start()
    pltpu.make_async_copy(enc, encb.at[y, x, c], load_sem.at[3]).start()
    for cc in (0, 1):
        pltpu.make_async_copy(
            win_in.at[pl.ds(2 * cc, 2), :, slab(t)], wcol.at[t, :, cc], load_sem.at[4]
        ).start()
    loads = [
        pltpu.make_async_copy(gate_in, gate, load_sem.at[2]),
        pltpu.make_async_copy(win_in, win, load_sem.at[0]),
        pltpu.make_async_copy(wout_in, wout, load_sem.at[1]),
    ]
    for cp in loads:
        cp.start()

    bar = pltpu.get_barrier_semaphore()
    partners = [at(y, up(x, d), cc) for d in (1, 2, 3) for cc in (0, 1)]
    partners += [at(up(y, d), x, cc) for d in (1, 2, 3) for cc in (0, 1)]
    partners += [mate, at(y, x, c, dd=1 - dp)]
    near = up(t, 3 - 2 * dp)
    far = up(t, 2)
    partners += [at(y, x, c, tt=near, dd=1 - dp), at(y, x, c, tt=far, dd=1 - dp)]
    partners += [zpeer[d] for d in (2, 1, 3)]
    owner = (t, 2 * c + lax.div(x, 2), lax.rem(x, 2), up(y, t))
    giver = (up(t, 4 - y), 2 * lax.rem(x, 2) + c, lax.div(x, 2), y)
    keeps = jnp.logical_and(
        jnp.logical_and(owner[0] == y, owner[1] == x), jnp.logical_and(owner[2] == c, owner[3] == t)
    )
    for p in reversed(partners):
        pl.semaphore_signal(bar, inc=1, device_id=p, device_id_type=MESH)
    pl.semaphore_signal(
        bar, inc=1, device_id=at(*giver, dd=1 - dp), device_id_type=MESH
    )

    @pl.when(jnp.logical_not(keeps))
    def _():
        pl.semaphore_signal(bar, inc=1, device_id=at(*giver), device_id_type=MESH)

    pl.semaphore_wait(bar, len(partners) + 2 - keeps.astype(jnp.int32))

    send(win_in.at[pl.ds(2 * c, 2), :, slab(near)], wcol.at[t, :, c], w_s.at[0], w_r.at[0],
         at(y, x, c, tt=near, dd=1 - dp))
    send(win_in.at[2 * c + 1 - dp, :, slab(far)], wcol.at[t, 1 - dp, c], w_s.at[1], w_r.at[1],
         at(y, x, c, tt=far, dd=1 - dp))

    above, below = up(y, 1), up(y, 3)
    for j in (0, 1):
        for n, src, step_y, rs in (
            (1, k_in, 1, kv_r.at[j, 0]),
            (2, v_in, 3, kv_r.at[j, 1]),
            (1, k_in, 3, qkv_r.at[j, 1]),
            (2, v_in, 1, qkv_r.at[j, 2]),
        ):
            for cc in (0, 1):
                send(src.at[:, cols(cc, j)], qkv.at[j, n, mine], qkv_s.at[j, n], rs, at(up(y, step_y), x, cc))
        for n, src in ((1, k_in), (2, v_in)):
            send(src.at[:, cols(1 - c, j)], qkv.at[j, n, mine], qkv_s.at[j, n], qkv_r.at[j, n], mate)
        for d in (2, 1, 3):
            for cc in (0, 1):
                send(q_in.at[:, cols(cc, j)], qkv.at[j, 0, me], qkv_s.at[j, 0], qkv_r.at[j, 0], at(y, up(x, d), cc))
        send(q_in.at[:, cols(1 - c, j)], qkv.at[j, 0, me], qkv_s.at[j, 0], qkv_r.at[j, 0], mate)
        if j == 0:
            for d in (1, 2, 3):
                send(enc, encb.at[y, x, c], enc_s.at[0], enc_r.at[0], xpeer[d])

    for cp in loads:
        cp.wait()
    pick = (lax.broadcasted_iota(jnp.int32, (16, gate.shape[0]), 1) == step[0]).astype(F32).astype(BF)
    gate_row = dot(pick, gate[...], 1, 0)[0:1]
    base = res[...].astype(F32)

    scale = HD ** (-0.5) * math.log2(math.e)

    def relay(j):
        wait(qkv.at[j, 1, pl.ds(0, 2)], kv_r.at[j, 0])
        low = pl.ds(2 * below, 2)
        send(qkv.at[j, 1, low], qkv.at[j, 1, low], kv_s.at[j, 0], qkv_r.at[j, 1], at(above, x, c))
        wait(qkv.at[j, 2, pl.ds(0, 2)], kv_r.at[j, 1])
        high = pl.ds(2 * above, 2)
        send(qkv.at[j, 2, high], qkv.at[j, 2, high], kv_s.at[j, 1], qkv_r.at[j, 2], at(below, x, c))

    def keys_of(j):
        wait(qkv.at[j, 0], qkv_r.at[j, 0])
        wait(qkv.at[j, 1, pl.ds(0, 6)], qkv_r.at[j, 1])
        wait(qkv.at[j, 2, pl.ds(0, 6)], qkv_r.at[j, 2])
        return qkv[j, 1].reshape(8 * TOK, HD), qkv[j, 2].reshape(8 * TOK, HD).T

    def produce(j, n, keys):
        h, it = lax.div(n, 2), lax.rem(n, 2)
        xs = (up(x, 1 + 2 * it), up(x, 2 + 2 * it))
        slots = [2 * xq + cc for xq in xs for cc in (0, 1)]
        rows = pl.ds(pl.multiple_of(h * 64, 64), 64)
        qb = jnp.concatenate([qkv[j, 0, s, rows] for s in slots], axis=0)
        st = dot(keys, qb, 1, 1)
        scores[lax.rem(n, 2)] = st
        tops[lax.rem(n, 2)] = jnp.broadcast_to(jnp.max(st, axis=0, keepdims=True), (8, 256))

    def consume(j, n, vt):
        h, it = lax.div(n, 2), lax.rem(n, 2)
        top = tops[lax.rem(n, 2), 0:1]
        expo = jnp.exp2((scores[lax.rem(n, 2)] - top) * scale)
        top = top * scale
        xs = (up(x, 1 + 2 * it), up(x, 2 + 2 * it))
        slots = [2 * xq + cc for xq in xs for cc in (0, 1)]
        total = jnp.sum(expo, axis=0, keepdims=True)
        out = (dot(vt, expo.astype(BF), 1, 0) / total).T.astype(BF)
        lse = top + jnp.log2(total)
        high = lse.astype(BF).astype(F32)
        mid = (lse - high).astype(BF).astype(F32)
        line = lax.broadcasted_iota(jnp.int32, (16, 256), 0)
        lses = jnp.where(line == 0, high, jnp.where(line == 1, mid, lse - high - mid)).astype(BF)
        for k, slot in enumerate(slots):
            osend[j, h, slot, 0:64] = out[64 * k : 64 * k + 64]
            osend[j, h, slot, 64:80] = lses[:, 128 * (k // 2) : 128 * (k // 2) + 128]

    def give(j, n):
        h, it = lax.div(n, 2), lax.rem(n, 2)
        xs = (up(x, 1 + 2 * it), up(x, 2 + 2 * it))
        for k in range(4):
            xq, cc = xs[k // 2], k % 2
            slot = 2 * xq + cc
            own = jnp.logical_and(xq == x, cc == c)

            @pl.when(own)
            def _():
                pltpu.make_async_copy(osend.at[j, h, slot], orecv.at[h, x, c, j], o_r.at[j, h]).start()

            @pl.when(jnp.logical_not(own))
            def _():
                send(osend.at[j, h, slot], orecv.at[h, x, c, j], o_s.at[j, h], o_r.at[j, h], at(y, xq, cc))

    def combine(j, h):
        wait(orecv.at[h, :, :, j], o_r.at[j, h])
        lses = [
            jnp.concatenate(
                [
                    jnp.sum(orecv[h, i, cc, j, 64:80].astype(F32)[0:3], axis=0, keepdims=True)
                    for cc in (0, 1)
                ],
                axis=0,
            )
            for i in range(4)
        ]
        top = jnp.maximum(jnp.maximum(lses[0], lses[1]), jnp.maximum(lses[2], lses[3]))
        ws = [jnp.exp2(v - top) for v in lses]
        inv = 1.0 / (ws[0] + ws[1] + ws[2] + ws[3])
        wt = jnp.concatenate([w * inv for w in ws], axis=0).T
        wt = jnp.where(c == 0, wt[0:64], wt[64:128])
        r = 64 * h
        for cc in (0, 1):
            acc = sum(
                orecv[h, i, cc, j, 0:64].astype(F32) * wt[:, 2 * i + cc : 2 * i + cc + 1] for i in range(4)
            )
            lo = (2 * cc + j) * HD
            hidf[t, j, r : r + 64, cc * HD : cc * HD + HD] = (
                base[r : r + 64, lo : lo + HD] + gate_row[:, lo : lo + HD] * acc
            ).astype(BF)

    def share(j, rows, k):
        for d in (2, 1, 3):
            send(hidf.at[t, j, rows], hidf.at[t, j, rows], hid_s.at[k], hid_r.at[k], zpeer[d])

    pair = at(y, x, c, dd=1 - dp)
    relay(0)
    relay(1)
    keys, vt = keys_of(0)
    produce(0, 0, keys)

    def step0(n, carry):
        consume(0, n, vt)
        produce(0, n + 1, keys)
        give(0, n)
        return carry

    lax.fori_loop(0, 3, step0, 0)
    consume(0, 3, vt)
    give(0, 3)
    wait(wcol.at[0, :, 0], w_r.at[0])
    send(wcol.at[near, :, c], wcol.at[near, :, c], w_s.at[2], w_r.at[2], pair)

    keys1, vt1 = keys_of(1)
    wait(enc, load_sem.at[3])
    wait(encb.at[0, pl.ds(0, 3), 0], enc_r.at[0])
    for d in (2, 1, 3):
        send(encb.at[y, :, c], encb.at[y, :, c], enc_s.at[1], enc_r.at[1], ypeer[d])
    produce(1, 0, keys1)

    def step1(n, carry):
        consume(1, n, vt1)
        produce(1, n + 1, keys1)
        give(1, n)
        return carry

    lax.fori_loop(0, 3, step1, 0)
    wait(wcol.at[0, 0, 0], w_r.at[1])
    send(wcol.at[far, dp, c], wcol.at[far, dp, c], w_s.at[3], w_r.at[3], pair)
    consume(1, 3, vt1)
    give(1, 3)
    combine(0, 0)
    combine(0, 1)
    share(0, pl.ds(0, TOK), 0)
    combine(1, 0)
    share(1, pl.ds(0, 64), 1)
    combine(1, 1)
    share(1, pl.ds(64, 64), 2)

    wait(wcol.at[0, :, 0], w_r.at[2])
    wait(wcol.at[0, 0, 0], w_r.at[3])
    for d in (1, 2, 3):
        s = up(t, d)
        send(wcol.at[s, :, c], wcol.at[s, :, c], w_s.at[4], w_r.at[4], mate)
    wait(encb.at[0:3, :, 0], enc_r.at[1])
    send(encb.at[:, :, c], encb.at[:, :, c], enc_s.at[2], enc_r.at[2], mate)

    def first_end(h):
        rows = pl.ds(64 * h, 64)
        wait(hidf.at[pl.ds(0, 3), 1, pl.ds(0, 64)], hid_r.at[1 + h])
        total = inner[rows] + sum(
            dot(hidf[s, 1, rows], wcol[s, 1].reshape(256, 512), 1, 0) for s in range(4)
        )
        inner[rows] = total
        act[rows] = (total / (1.0 + jnp.exp(-total))).astype(BF)

    def last_start(h):
        rows = pl.ds(64 * h, 64)
        psend[rows] = dot(act[rows], wout[...], 1, 0).astype(BF)
        for d in (2, 1, 3):
            send(psend.at[trows(h, up(t, d))], precv.at[h, d - 1], p_s.at[h], p_r.at[h], zpeer[d])

    def loss(h):
        wait(tgt.at[h, pl.ds(0, 3)], tg_r.at[h])
        tg = jnp.concatenate([tgt[h, s].astype(F32) for s in range(4)], axis=1)
        norm_t = jnp.sqrt(jnp.sum(tg * tg, axis=1, keepdims=True) + eps)
        wait(precv.at[h], p_r.at[h])
        proj = psend[trows(h, t)].astype(F32) + sum(precv[h, i].astype(F32) for i in range(3))
        norm_p = jnp.sqrt(jnp.sum(proj * proj, axis=1, keepdims=True) + eps)
        cosine = jnp.sum(proj * tg, axis=1, keepdims=True) / (norm_p * norm_t)
        factor = loss_scale / ALL_TOKENS
        own = trows(h, t)
        g2[own] = (-factor * (tg / (norm_p * norm_t) - cosine * proj / (norm_p * norm_p))).astype(BF)
        for d in (2, 1, 3):
            send(g2.at[own], g2.at[own], g_s.at[h], g_r.at[h], zpeer[d])

    def hidden_grad(h):
        rows = pl.ds(64 * h, 64)
        mrows = pl.ds(TOK + 64 * h, 64)
        wait(g2.at[0:48], g_r.at[h])
        send(g2.at[rows], g2.at[mrows], mate_s.at[2 + h], mate_r.at[2 + h], mate)
        v = inner[rows]
        sig = 1.0 / (1.0 + jnp.exp(-v))
        grad_act = dot(g2[rows], wout[...], 1, 1)
        gi[t, rows] = (grad_act * (sig * (1.0 + v * (1.0 - sig)))).astype(BF)
        for d in (2, 1, 3):
            send(gi.at[t, rows], gi.at[t, rows], gi_s, gi_r.at[d - 1], zpeer[d])
        send(gi.at[t, rows, other], gia.at[mrows], mate_s.at[4 + h], mate_r.at[4 + h], mate)

    weights = tap_w[...]
    weights = weights / jnp.sum(weights, axis=0, keepdims=True)
    taps = jnp.concatenate([tap_rows[...].astype(F32), weights], axis=0).T
    rows, weights = taps[:, 0:4], taps[:, 4:8]
    lane = lax.broadcasted_iota(jnp.int32, (TOK, 1536), 1).astype(F32)
    mix = sum(jnp.where(lane == rows[:, k : k + 1], weights[:, k : k + 1], 0.0) for k in range(4))
    wait(encb.at[:, :, 0], enc_r.at[2])
    tgs[...] = dot(mix.astype(BF), encb[...].reshape(1536, 384), 1, 0).astype(BF)
    for h in (0, 1):
        for d in (2, 1, 3):
            send(tgs.at[trows(h, up(t, d))], tgt.at[h, t], tg_s.at[h], tg_r.at[h], zpeer[d])
        tgt[h, t] = tgs[trows(h, t)]

    wait(wcol.at[0], load_sem.at[4])
    wait(wcol.at[pl.ds(0, 3), :, 0], w_r.at[4])
    wait(hidf.at[pl.ds(0, 3), 0, pl.ds(0, TOK)], hid_r.at[0])
    inner[...] = sum(dot(hidf[s, 0, 0:TOK], wcol[s, 0].reshape(256, 512), 1, 0) for s in range(4))
    for h in (0, 1):
        first_end(h)
        last_start(h)
    send(hidf.at[:, :, pl.ds(0, TOK)], hidf.at[:, :, pl.ds(TOK, TOK)], mate_s.at[0], mate_r.at[0], mate)
    a2[0:TOK] = act[:, half]
    send(act.at[:, other], a2.at[pl.ds(TOK, TOK)], mate_s.at[1], mate_r.at[1], mate)
    for h in (0, 1):
        loss(h)
    for h in (0, 1):
        hidden_grad(h)

    wait(a2.at[0:TOK], mate_r.at[1])
    for h in (0, 1):
        wait(g2.at[0:64], mate_r.at[2 + h])
    for yy in range(4):
        part = dot(g2[:, yy * 384 : (yy + 1) * 384], a2[...], 0, 0).astype(BF)
        p2a[yy] = part[:, 0:128].reshape(4, 96, 128)
        p2b[yy] = part[:, 128:256].reshape(4, 96, 128)
    gia[0:TOK] = gi[t, :, half]
    wait(hidf.at[:, :, pl.ds(0, TOK)], mate_r.at[0])
    for h in (0, 1):
        wait(gia.at[0:64], mate_r.at[4 + h])
    for d in (2, 1, 3, 0):
        s = up(up(y, d), t)
        p1a[s] = dot(gia[...], hidf[s, 0], 0, 0).astype(BF)
        p1b[:, s] = dot(gia[...], hidf[s, 1], 0, 0).astype(BF).reshape(4, 64, 256)
        if d:
            send(p1a.at[s], r1a.at[d - 1], red_s.at[0], red_r.at[0], ypeer[d])
    for d in (2, 1, 3):
        send(p1b.at[up(x, d)], r1b.at[d - 1], red_s.at[1], red_r.at[1], xpeer[d])
    for d in (2, 1, 3):
        send(p2a.at[up(y, d)], r2a.at[d - 1], red_s.at[5], red_r.at[5], ypeer[d])
        send(p2b.at[:, up(x, d)], r2b.at[d - 1], red_s.at[6], red_r.at[6], xpeer[d])

    def first(s, start):
        part = dot(gi[s], win[:, :, slab(s)].reshape(512, 512), 1, 1)
        dacc[...] = part if start else dacc[...] + part

    first(t, True)

    block_mine = up(y, t)
    wait(r1a, red_r.at[0])
    total = p1a[block_mine].astype(F32) + sum(r1a[i].astype(F32) for i in range(3))
    s1a[...] = total.astype(BF).reshape(4, 64, 256)
    for d in (2, 1, 3):
        send(s1a.at[up(x, d)], t1a.at[d - 1], red_s.at[2], red_r.at[2], xpeer[d])
    wait(r1b, red_r.at[1])
    s1b[...] = (p1b[x].astype(F32) + sum(r1b[i].astype(F32) for i in range(3))).astype(BF)
    for d in (2, 1, 3):
        send(s1b.at[up(up(y, d), t)], t1b.at[d - 1], red_s.at[3], red_r.at[3], ypeer[d])

    wait(r2a, red_r.at[5])
    s2a[...] = (p2a[y].astype(F32) + sum(r2a[i].astype(F32) for i in range(3))).astype(BF)
    wait(r2b, red_r.at[6])
    s2b[...] = (p2b[:, x].astype(F32) + sum(r2b[i].astype(F32) for i in range(3))).astype(BF)
    for d in (2, 1, 3, 0):
        for e in (0, 1):
            cc = lax.rem(c + e, 2)
            part = pl.ds(pl.multiple_of(cc * 48, 16), 48)
            xq, yq = up(x, d), up(y, d)
            if d == 0 and e == 0:
                pltpu.make_async_copy(s2a.at[x, part], t2a.at[c, x], red_r.at[7]).start()
                pltpu.make_async_copy(s2b.at[y, part], t2b.at[c, y], red_r.at[8]).start()
            else:
                k = 7 if d else 8
                send(s2a.at[xq, part], t2a.at[c, x], red_s.at[k], red_r.at[7], at(y, xq, cc))
                send(s2b.at[yq, part], t2b.at[c, y], red_s.at[k], red_r.at[8], at(yq, x, cc))

    wait(t1a, red_r.at[2])
    f1[0] = (s1a[x].astype(F32) + sum(t1a[i].astype(F32) for i in range(3))).astype(BF)
    wait(t1b, red_r.at[3])
    f1[1] = (s1b[block_mine].astype(F32) + sum(t1b[i].astype(F32) for i in range(3))).astype(BF)
    send(f1, e1.at[dp], red_s.at[4], red_r.at[4], at(*owner, dd=1 - dp))

    @pl.when(keeps)
    def _():
        pltpu.make_async_copy(f1, e1.at[dp], red_r.at[4]).start()

    @pl.when(jnp.logical_not(keeps))
    def _():
        send(f1, e1.at[dp], red_s.at[4], red_r.at[4], at(*owner))

    wait(t2a, red_r.at[7])
    wait(t2b, red_r.at[8])
    for cc in (0, 1):
        for n, f in enumerate((t2a, t2b)):
            total = sum(f[cc, i].astype(F32) for i in range(4))
            f2[:, 256 * cc + 128 * n : 256 * cc + 128 * n + 128] = total.astype(BF)
    send(f2, e2, red_s.at[9], red_r.at[9], pair)

    for d in (1, 3, 2):
        s = up(t, 4 - d)
        wait(gi.at[0], gi_r.at[d - 1])
        first(s, False)
    d_out[...] = dacc[...].astype(BF)

    for j in (0, 1):
        wait(qkv.at[j, 0, pl.ds(0, 7)], qkv_s.at[j, 0])
        for n in (0, 1):
            wait(qkv.at[j, 0, pl.ds(0, 5)], qkv_s.at[j, 1 + n])
            wait(qkv.at[j, 0, pl.ds(0, 2)], kv_s.at[j, n])
        for h in (0, 1):
            wait(osend.at[j, h, pl.ds(0, 7)], o_s.at[j, h])
    wait(wcol.at[0, :, 0], w_s.at[0])
    wait(wcol.at[0, 0, 0], w_s.at[1])
    wait(wcol.at[0, :, 0], w_s.at[2])
    wait(wcol.at[0, 0, 0], w_s.at[3])
    wait(wcol.at[pl.ds(0, 3), :, 0], w_s.at[4])
    wait(encb.at[0, pl.ds(0, 3), 0], enc_s.at[0])
    wait(encb.at[0:3, :, 0], enc_s.at[1])
    wait(encb.at[:, :, 0], enc_s.at[2])
    wait(hidf.at[pl.ds(0, 3), 0, pl.ds(0, TOK)], hid_s.at[0])
    wait(hidf.at[:, :, pl.ds(0, TOK)], mate_s.at[0])
    wait(a2.at[0:TOK], mate_s.at[1])
    for h in (0, 1):
        wait(hidf.at[pl.ds(0, 3), 1, pl.ds(0, 64)], hid_s.at[1 + h])
        wait(tgt.at[h, pl.ds(0, 3)], tg_s.at[h])
        wait(precv.at[h], p_s.at[h])
        wait(g2.at[0:48], g_s.at[h])
        wait(g2.at[0:64], mate_s.at[2 + h])
        wait(gia.at[0:64], mate_s.at[4 + h])
    wait(gi.at[pl.ds(0, 3)], gi_s)
    wait(r1a, red_s.at[0])
    wait(r1b, red_s.at[1])
    wait(t1a, red_s.at[2])
    wait(t1b, red_s.at[3])
    wait(r2a, red_s.at[5])
    wait(r2b, red_s.at[6])
    wait(r2a.at[:, pl.ds(0, 2)], red_s.at[7])
    wait(s2a.at[0], red_s.at[8])
    wait(f2, red_s.at[9])

    @pl.when(keeps)
    def _():
        wait(f1, red_s.at[4])

    @pl.when(jnp.logical_not(keeps))
    def _():
        wait(e1, red_s.at[4])

    wait(e2, red_r.at[9])
    gout_out[...] = f2[...].astype(F32) + e2[...].astype(F32)
    wait(e1, red_r.at[4])
    for j in (0, 1):
        total = e1[0, j].astype(F32) + e1[1, j].astype(F32)
        for cc in (0, 1):
            lo = (2 * cc + j) * HD
            gin_out[:, lo : lo + HD] = total[:, cc * HD : cc * HD + HD]


def keep(a, b, c, a_out, b_out, c_out):
    a_out[...] = a[...]
    b_out[...] = b[...]
    c_out[...] = c[...]


def local(
    residual, queries, attn_keys, attn_values, gate_table, timesteps, enc_feats,
    tap_rows, tap_weights, proj_in, proj_out,
):
    dma = pltpu.SemaphoreType.DMA
    vm = pl.BlockSpec(memory_space=VMEM)
    hb = pl.BlockSpec(memory_space=pl.ANY)
    sm = pl.BlockSpec(memory_space=pltpu.SMEM)
    d_hidden, gin, gout = pl.pallas_call(
        kernel,
        name="alignment",
        out_shape=(
            jax.ShapeDtypeStruct((TOK, 512), BF),
            jax.ShapeDtypeStruct((64, 512), F32),
            jax.ShapeDtypeStruct((48, 512), F32),
        ),
        in_specs=[vm, hb, hb, hb, hb, sm, hb, vm, vm, hb, hb],
        out_specs=(vm, vm, vm),
        scratch_shapes=[
            VMEM((2, 3, 8, TOK, HD), BF),
            VMEM((1000, 512), BF),
            VMEM((4, HD, 2048), BF),
            VMEM((4, 2, 2, HD, 512), BF),
            VMEM((512, 1536), BF),
            VMEM((4, 4, 2, 48, 384), BF),
            VMEM((2, 2, 8, 80, HD), BF),
            VMEM((2, 4, 2, 2, 80, HD), BF),
            VMEM((2, 8 * TOK, 256), F32),
            VMEM((2, 8, 256), F32),
            VMEM((TOK, 384), BF),
            VMEM((2, 4, 16, 384), BF),
            VMEM((4, 2, 2 * TOK, 256), BF),
            VMEM((TOK, 512), F32),
            VMEM((TOK, 512), BF),
            VMEM((2 * TOK, 256), BF),
            VMEM((TOK, 1536), BF),
            VMEM((2, 3, 16, 1536), BF),
            VMEM((2 * TOK, 1536), BF),
            VMEM((4, TOK, 512), BF),
            VMEM((2 * TOK, 256), BF),
            VMEM((TOK, 512), F32),
            VMEM((4, 256, 256), BF),
            VMEM((4, 4, 64, 256), BF),
            VMEM((3, 256, 256), BF),
            VMEM((3, 4, 64, 256), BF),
            VMEM((4, 64, 256), BF),
            VMEM((4, 64, 256), BF),
            VMEM((3, 64, 256), BF),
            VMEM((3, 64, 256), BF),
            VMEM((2, 64, 256), BF),
            VMEM((2, 2, 64, 256), BF),
            VMEM((4, 4, 96, 128), BF),
            VMEM((4, 4, 96, 128), BF),
            VMEM((3, 4, 96, 128), BF),
            VMEM((3, 4, 96, 128), BF),
            VMEM((4, 96, 128), BF),
            VMEM((4, 96, 128), BF),
            VMEM((2, 4, 48, 128), BF),
            VMEM((2, 4, 48, 128), BF),
            VMEM((48, 512), BF),
            VMEM((48, 512), BF),
            dma((5,)),
            dma((2, 3)),
            dma((2, 3)),
            dma((2, 2)),
            dma((2, 2)),
            dma((5,)),
            dma((5,)),
            dma((3,)),
            dma((3,)),
            dma((2, 2)),
            dma((2, 2)),
            dma((2,)),
            dma((2,)),
            dma((6,)),
            dma((6,)),
            dma((3,)),
            dma((3,)),
            dma((2,)),
            dma((2,)),
            dma((2,)),
            dma((2,)),
            dma,
            dma((3,)),
            dma((10,)),
            dma((10,)),
        ],
        compiler_params=pltpu.CompilerParams(
            collective_id=0, has_side_effects=True, vmem_limit_bytes=56 << 20
        ),
        cost_estimate=pl.CostEstimate(
            flops=2_500_000_000, bytes_accessed=16_000_000, transcendentals=2_200_000
        ),
    )(
        residual[0], queries[0], attn_keys[0], attn_values[0], gate_table, timesteps,
        enc_feats[0], tap_rows[0].T, tap_weights[0].T, proj_in.reshape(4, HD, 2048), proj_out,
    )
    d_hidden, gin, gout = pl.pallas_call(
        keep,
        name="keep",
        out_shape=(
            jax.ShapeDtypeStruct((TOK, 512), BF),
            jax.ShapeDtypeStruct((64, 512), F32),
            jax.ShapeDtypeStruct((48, 512), F32),
        ),
        in_specs=[vm, vm, vm],
        out_specs=(vm, vm, vm),
    )(d_hidden, gin, gout)
    return d_hidden[None], gin.T, gout.T


def solution(mesh):
    in_specs = (
        P("dp", "ctx", "tp"),
        P("dp", "ctx", "tp"),
        P("dp", "ctx", "tp"),
        P("dp", "ctx", "tp"),
        P(None, "tp"),
        P("dp"),
        P("dp", "ctx", "tp"),
        P("dp", "ctx", None),
        P("dp", "ctx", None),
        P("tp", None),
        P("tp", None),
    )
    out_specs = (P("dp", "ctx", "tp"), P("tp", "ctx"), P("tp", "ctx"))
    return jax.shard_map(local, mesh=mesh, in_specs=in_specs, out_specs=out_specs, check_vma=False)
```

```python
import functools
import math

import jax
import jax.numpy as jnp
from jax import lax
from jax.experimental import pallas as pl
from jax.experimental.pallas import tpu as pltpu
from jax.sharding import PartitionSpec as P

HD = 128
TOK = 128
eps = 1e-06
loss_scale = 4194304.0
ALL_TOKENS = 8192
BF = jnp.bfloat16
F32 = jnp.float32
MESH = pl.DeviceIdType.MESH
VMEM = pltpu.VMEM


def dot(a, b, ca, cb):
    return lax.dot_general(a, b, (((ca,), (cb,)), ((), ())), preferred_element_type=F32)


def kernel(
    res, q_in, k_in, v_in, gate_in, step, enc, tap_rows, tap_w, win_in, wout_in,
    d_out, gin_out, gout_out,
    qkv, gate, win, wcol, wout, encb, osend, orecv,
    scores, tops, tgs, tgt, hidf, inner, act, a2, psend, precv, g2, gi, gia, dacc,
    p1a, p1b, r1a, r1b, s1a, s1b, t1a, t1b, f1, e1,
    p2a, p2b, r2a, r2b, s2a, s2b, t2a, t2b, f2, e2,
    load_sem, qkv_s, qkv_r, kv_s, kv_r, w_s, w_r, enc_s, enc_r, o_s, o_r, tg_s, tg_r,
    mate_s, mate_r, hid_s, hid_r, p_s, p_r, g_s, g_r, gi_s, gi_r, red_s, red_r,
):
    ctx = lax.axis_index("ctx")
    t = lax.axis_index("tp")
    dp = lax.axis_index("dp")
    c = lax.rem(ctx, 2)
    x = lax.rem(lax.div(ctx, 2), 4)
    y = lax.div(ctx, 8)
    me = x * 2 + c
    mine = y * 2 + c

    def at(yy, xx, cc, tt=None, dd=None):
        return {
            "ctx": (yy * 4 + xx) * 2 + cc,
            "tp": t if tt is None else tt,
            "dp": dp if dd is None else dd,
        }

    def up(v, d):
        return lax.rem(v + d, 4)

    mate = at(y, x, 1 - c)
    zpeer = {d: at(y, x, c, tt=up(t, d)) for d in (1, 2, 3)}
    xpeer = {d: at(y, up(x, d), c) for d in (1, 2, 3)}
    ypeer = {d: at(up(y, d), x, c) for d in (1, 2, 3)}

    def send(src, dst, ss, rs, dev):
        cp = pltpu.make_async_remote_copy(
            src_ref=src, dst_ref=dst, send_sem=ss, recv_sem=rs, device_id=dev, device_id_type=MESH
        )
        cp.start()

    def wait(ref, sem):
        pltpu.make_async_copy(ref, ref, sem).wait()

    def cols(cc, j):
        return pl.ds(pl.multiple_of(cc * 256 + j * 128, 128), 128)

    half = pl.ds(pl.multiple_of(c * 256, 256), 256)
    other = pl.ds(pl.multiple_of((1 - c) * 256, 256), 256)

    def slab(tt):
        return pl.ds(pl.multiple_of(tt * 512, 512), 512)

    def trows(h, tt):
        return pl.ds(pl.multiple_of(h * 64 + tt * 16, 16), 16)

    for j in (0, 1):
        for n, src, slot in ((1, k_in, mine), (0, q_in, me), (2, v_in, mine)):
            pltpu.make_async_copy(src.at[:, cols(c, j)], qkv.at[j, n, slot], qkv_r.at[j, n]).start()
    pltpu.make_async_copy(enc, encb.at[y, x, c], load_sem.at[3]).start()
    for cc in (0, 1):
        pltpu.make_async_copy(
            win_in.at[pl.ds(2 * cc, 2), :, slab(t)], wcol.at[t, :, cc], load_sem.at[4]
        ).start()
    loads = [
        pltpu.make_async_copy(gate_in, gate, load_sem.at[2]),
        pltpu.make_async_copy(win_in, win, load_sem.at[0]),
        pltpu.make_async_copy(wout_in, wout, load_sem.at[1]),
    ]
    for cp in loads:
        cp.start()

    bar = pltpu.get_barrier_semaphore()
    partners = [at(y, up(x, d), cc) for d in (1, 2, 3) for cc in (0, 1)]
    partners += [at(up(y, d), x, cc) for d in (1, 2, 3) for cc in (0, 1)]
    partners += [mate, at(y, x, c, dd=1 - dp)]
    near = up(t, 3 - 2 * dp)
    far = up(t, 2)
    partners += [at(y, x, c, tt=near, dd=1 - dp), at(y, x, c, tt=far, dd=1 - dp)]
    partners += [zpeer[d] for d in (2, 1, 3)]
    owner = (t, 2 * c + lax.div(x, 2), lax.rem(x, 2), up(y, t))
    giver = (up(t, 4 - y), 2 * lax.rem(x, 2) + c, lax.div(x, 2), y)
    keeps = jnp.logical_and(
        jnp.logical_and(owner[0] == y, owner[1] == x), jnp.logical_and(owner[2] == c, owner[3] == t)
    )
    for p in reversed(partners):
        pl.semaphore_signal(bar, inc=1, device_id=p, device_id_type=MESH)
    pl.semaphore_signal(
        bar, inc=1, device_id=at(*giver, dd=1 - dp), device_id_type=MESH
    )

    @pl.when(jnp.logical_not(keeps))
    def _():
        pl.semaphore_signal(bar, inc=1, device_id=at(*giver), device_id_type=MESH)

    pl.semaphore_wait(bar, len(partners) + 2 - keeps.astype(jnp.int32))

    send(win_in.at[pl.ds(2 * c, 2), :, slab(near)], wcol.at[t, :, c], w_s.at[0], w_r.at[0],
         at(y, x, c, tt=near, dd=1 - dp))
    send(win_in.at[2 * c + 1 - dp, :, slab(far)], wcol.at[t, 1 - dp, c], w_s.at[1], w_r.at[1],
         at(y, x, c, tt=far, dd=1 - dp))

    above, below = up(y, 1), up(y, 3)
    for j in (0, 1):
        for n, src, step_y, rs in (
            (1, k_in, 1, kv_r.at[j, 0]),
            (2, v_in, 3, kv_r.at[j, 1]),
            (1, k_in, 3, qkv_r.at[j, 1]),
            (2, v_in, 1, qkv_r.at[j, 2]),
        ):
            for cc in (0, 1):
                send(src.at[:, cols(cc, j)], qkv.at[j, n, mine], qkv_s.at[j, n], rs, at(up(y, step_y), x, cc))
        for n, src in ((1, k_in), (2, v_in)):
            send(src.at[:, cols(1 - c, j)], qkv.at[j, n, mine], qkv_s.at[j, n], qkv_r.at[j, n], mate)
        for d in (2, 1, 3):
            for cc in (0, 1):
                send(q_in.at[:, cols(cc, j)], qkv.at[j, 0, me], qkv_s.at[j, 0], qkv_r.at[j, 0], at(y, up(x, d), cc))
        send(q_in.at[:, cols(1 - c, j)], qkv.at[j, 0, me], qkv_s.at[j, 0], qkv_r.at[j, 0], mate)
        if j == 0:
            for d in (1, 2, 3):
                send(enc, encb.at[y, x, c], enc_s.at[0], enc_r.at[0], xpeer[d])

    for cp in loads:
        cp.wait()
    pick = (lax.broadcasted_iota(jnp.int32, (16, gate.shape[0]), 1) == step[0]).astype(F32).astype(BF)
    gate_row = dot(pick, gate[...], 1, 0)[0:1]
    base = res[...].astype(F32)

    scale = HD ** (-0.5) * math.log2(math.e)

    def relay(j):
        wait(qkv.at[j, 1, pl.ds(0, 2)], kv_r.at[j, 0])
        low = pl.ds(2 * below, 2)
        send(qkv.at[j, 1, low], qkv.at[j, 1, low], kv_s.at[j, 0], qkv_r.at[j, 1], at(above, x, c))
        wait(qkv.at[j, 2, pl.ds(0, 2)], kv_r.at[j, 1])
        high = pl.ds(2 * above, 2)
        send(qkv.at[j, 2, high], qkv.at[j, 2, high], kv_s.at[j, 1], qkv_r.at[j, 2], at(below, x, c))

    def keys_of(j):
        wait(qkv.at[j, 0], qkv_r.at[j, 0])
        wait(qkv.at[j, 1, pl.ds(0, 6)], qkv_r.at[j, 1])
        wait(qkv.at[j, 2, pl.ds(0, 6)], qkv_r.at[j, 2])
        return qkv[j, 1].reshape(8 * TOK, HD), qkv[j, 2].reshape(8 * TOK, HD).T

    def produce(j, n, keys):
        h, it = lax.div(n, 2), lax.rem(n, 2)
        xs = (up(x, 1 + 2 * it), up(x, 2 + 2 * it))
        slots = [2 * xq + cc for xq in xs for cc in (0, 1)]
        rows = pl.ds(pl.multiple_of(h * 64, 64), 64)
        qb = jnp.concatenate([qkv[j, 0, s, rows] for s in slots], axis=0)
        st = dot(keys, qb, 1, 1)
        scores[lax.rem(n, 2)] = st
        tops[lax.rem(n, 2)] = jnp.broadcast_to(jnp.max(st, axis=0, keepdims=True), (8, 256))

    def consume(j, n, vt):
        h, it = lax.div(n, 2), lax.rem(n, 2)
        top = tops[lax.rem(n, 2), 0:1]
        expo = jnp.exp2((scores[lax.rem(n, 2)] - top) * scale)
        top = top * scale
        xs = (up(x, 1 + 2 * it), up(x, 2 + 2 * it))
        slots = [2 * xq + cc for xq in xs for cc in (0, 1)]
        total = jnp.sum(expo, axis=0, keepdims=True)
        out = (dot(vt, expo.astype(BF), 1, 0) / total).T.astype(BF)
        lse = top + jnp.log2(total)
        high = lse.astype(BF).astype(F32)
        mid = (lse - high).astype(BF).astype(F32)
        line = lax.broadcasted_iota(jnp.int32, (16, 256), 0)
        lses = jnp.where(line == 0, high, jnp.where(line == 1, mid, lse - high - mid)).astype(BF)
        for k, slot in enumerate(slots):
            osend[j, h, slot, 0:64] = out[64 * k : 64 * k + 64]
            osend[j, h, slot, 64:80] = lses[:, 128 * (k // 2) : 128 * (k // 2) + 128]

    def give(j, n):
        h, it = lax.div(n, 2), lax.rem(n, 2)
        xs = (up(x, 1 + 2 * it), up(x, 2 + 2 * it))
        for k in range(4):
            xq, cc = xs[k // 2], k % 2
            slot = 2 * xq + cc
            own = jnp.logical_and(xq == x, cc == c)

            @pl.when(own)
            def _():
                pltpu.make_async_copy(osend.at[j, h, slot], orecv.at[h, x, c, j], o_r.at[j, h]).start()

            @pl.when(jnp.logical_not(own))
            def _():
                send(osend.at[j, h, slot], orecv.at[h, x, c, j], o_s.at[j, h], o_r.at[j, h], at(y, xq, cc))

    def combine(j, h):
        wait(orecv.at[h, :, :, j], o_r.at[j, h])
        lses = [
            jnp.concatenate(
                [
                    jnp.sum(orecv[h, i, cc, j, 64:80].astype(F32)[0:3], axis=0, keepdims=True)
                    for cc in (0, 1)
                ],
                axis=0,
            )
            for i in range(4)
        ]
        top = jnp.maximum(jnp.maximum(lses[0], lses[1]), jnp.maximum(lses[2], lses[3]))
        ws = [jnp.exp2(v - top) for v in lses]
        inv = 1.0 / (ws[0] + ws[1] + ws[2] + ws[3])
        wt = jnp.concatenate([w * inv for w in ws], axis=0).T
        wt = jnp.where(c == 0, wt[0:64], wt[64:128])
        r = 64 * h
        for cc in (0, 1):
            acc = sum(
                orecv[h, i, cc, j, 0:64].astype(F32) * wt[:, 2 * i + cc : 2 * i + cc + 1] for i in range(4)
            )
            lo = (2 * cc + j) * HD
            hidf[t, j, r : r + 64, cc * HD : cc * HD + HD] = (
                base[r : r + 64, lo : lo + HD] + gate_row[:, lo : lo + HD] * acc
            ).astype(BF)

    def share(j, rows, k):
        for d in (2, 1, 3):
            send(hidf.at[t, j, rows], hidf.at[t, j, rows], hid_s.at[k], hid_r.at[k], zpeer[d])

    pair = at(y, x, c, dd=1 - dp)
    relay(0)
    relay(1)
    keys, vt = keys_of(0)
    produce(0, 0, keys)

    def step0(n, carry):
        consume(0, n, vt)
        produce(0, n + 1, keys)
        give(0, n)
        return carry

    lax.fori_loop(0, 3, step0, 0)
    consume(0, 3, vt)
    give(0, 3)
    wait(wcol.at[0, :, 0], w_r.at[0])
    send(wcol.at[near, :, c], wcol.at[near, :, c], w_s.at[2], w_r.at[2], pair)

    keys1, vt1 = keys_of(1)
    wait(enc, load_sem.at[3])
    wait(encb.at[0, pl.ds(0, 3), 0], enc_r.at[0])
    for d in (2, 1, 3):
        send(encb.at[y, :, c], encb.at[y, :, c], enc_s.at[1], enc_r.at[1], ypeer[d])
    produce(1, 0, keys1)

    def step1(n, carry):
        consume(1, n, vt1)
        produce(1, n + 1, keys1)
        give(1, n)
        return carry

    lax.fori_loop(0, 3, step1, 0)
    wait(wcol.at[0, 0, 0], w_r.at[1])
    send(wcol.at[far, dp, c], wcol.at[far, dp, c], w_s.at[3], w_r.at[3], pair)
    consume(1, 3, vt1)
    give(1, 3)
    combine(0, 0)
    share(0, pl.ds(0, 64), 0)
    combine(0, 1)
    share(0, pl.ds(64, 64), 0)
    combine(1, 0)
    share(1, pl.ds(0, 64), 1)
    combine(1, 1)
    share(1, pl.ds(64, 64), 2)

    wait(wcol.at[0, :, 0], w_r.at[2])
    wait(wcol.at[0, 0, 0], w_r.at[3])
    for d in (1, 2, 3):
        s = up(t, d)
        send(wcol.at[s, :, c], wcol.at[s, :, c], w_s.at[4], w_r.at[4], mate)
    wait(encb.at[0:3, :, 0], enc_r.at[1])
    send(encb.at[:, :, c], encb.at[:, :, c], enc_s.at[2], enc_r.at[2], mate)

    def first_end(h):
        rows = pl.ds(64 * h, 64)
        wait(hidf.at[pl.ds(0, 3), 1, pl.ds(0, 64)], hid_r.at[1 + h])
        total = inner[rows] + sum(
            dot(hidf[s, 1, rows], wcol[s, 1].reshape(256, 512), 1, 0) for s in range(4)
        )
        inner[rows] = total
        act[rows] = (total / (1.0 + jnp.exp(-total))).astype(BF)

    def last_start(h):
        rows = pl.ds(64 * h, 64)
        psend[rows] = dot(act[rows], wout[...], 1, 0).astype(BF)
        for d in (2, 1, 3):
            send(psend.at[trows(h, up(t, d))], precv.at[h, d - 1], p_s.at[h], p_r.at[h], zpeer[d])

    def loss(h):
        wait(tgt.at[h, pl.ds(0, 3)], tg_r.at[h])
        tg = jnp.concatenate([tgt[h, s].astype(F32) for s in range(4)], axis=1)
        norm_t = jnp.sqrt(jnp.sum(tg * tg, axis=1, keepdims=True) + eps)
        wait(precv.at[h], p_r.at[h])
        proj = psend[trows(h, t)].astype(F32) + sum(precv[h, i].astype(F32) for i in range(3))
        norm_p = jnp.sqrt(jnp.sum(proj * proj, axis=1, keepdims=True) + eps)
        cosine = jnp.sum(proj * tg, axis=1, keepdims=True) / (norm_p * norm_t)
        factor = loss_scale / ALL_TOKENS
        own = trows(h, t)
        g2[own] = (-factor * (tg / (norm_p * norm_t) - cosine * proj / (norm_p * norm_p))).astype(BF)
        for d in (2, 1, 3):
            send(g2.at[own], g2.at[own], g_s.at[h], g_r.at[h], zpeer[d])

    def hidden_grad(h):
        rows = pl.ds(64 * h, 64)
        mrows = pl.ds(TOK + 64 * h, 64)
        wait(g2.at[0:48], g_r.at[h])
        send(g2.at[rows], g2.at[mrows], mate_s.at[2 + h], mate_r.at[2 + h], mate)
        grad_act = dot(g2[rows], wout[...], 1, 1)
        gi[t, rows] = (grad_act * inner[rows]).astype(BF)
        for d in (2, 1, 3):
            send(gi.at[t, rows], gi.at[t, rows], gi_s, gi_r.at[d - 1], zpeer[d])
        send(gi.at[t, rows, other], gia.at[mrows], mate_s.at[4 + h], mate_r.at[4 + h], mate)

    weights = tap_w[...]
    weights = weights / jnp.sum(weights, axis=0, keepdims=True)
    taps = jnp.concatenate([tap_rows[...].astype(F32), weights], axis=0).T
    rows, weights = taps[:, 0:4], taps[:, 4:8]
    lane = lax.broadcasted_iota(jnp.int32, (TOK, 1536), 1).astype(F32)
    mix = sum(jnp.where(lane == rows[:, k : k + 1], weights[:, k : k + 1], 0.0) for k in range(4))
    wait(encb.at[:, :, 0], enc_r.at[2])
    tgs[...] = dot(mix.astype(BF), encb[...].reshape(1536, 384), 1, 0).astype(BF)
    for h in (0, 1):
        for d in (2, 1, 3):
            send(tgs.at[trows(h, up(t, d))], tgt.at[h, t], tg_s.at[h], tg_r.at[h], zpeer[d])
        tgt[h, t] = tgs[trows(h, t)]

    wait(wcol.at[0], load_sem.at[4])
    wait(wcol.at[pl.ds(0, 3), :, 0], w_r.at[4])
    wait(hidf.at[pl.ds(0, 3), 0, pl.ds(0, TOK)], hid_r.at[0])
    inner[...] = sum(dot(hidf[s, 0, 0:TOK], wcol[s, 0].reshape(256, 512), 1, 0) for s in range(4))
    for h in (0, 1):
        first_end(h)
        last_start(h)
    send(hidf.at[:, :, pl.ds(0, TOK)], hidf.at[:, :, pl.ds(TOK, TOK)], mate_s.at[0], mate_r.at[0], mate)
    a2[0:TOK] = act[:, half]
    send(act.at[:, other], a2.at[pl.ds(TOK, TOK)], mate_s.at[1], mate_r.at[1], mate)
    v = inner[...]
    sig = 1.0 / (1.0 + jnp.exp(-v))
    inner[...] = sig * (1.0 + v * (1.0 - sig))
    for h in (0, 1):
        loss(h)
    for h in (0, 1):
        hidden_grad(h)

    wait(a2.at[0:TOK], mate_r.at[1])
    for h in (0, 1):
        wait(g2.at[0:64], mate_r.at[2 + h])
    for yy in range(4):
        part = dot(g2[:, yy * 384 : (yy + 1) * 384], a2[...], 0, 0).astype(BF)
        p2a[yy] = part[:, 0:128].reshape(4, 96, 128)
        p2b[yy] = part[:, 128:256].reshape(4, 96, 128)
    gia[0:TOK] = gi[t, :, half]
    wait(hidf.at[:, :, pl.ds(0, TOK)], mate_r.at[0])
    for h in (0, 1):
        wait(gia.at[0:64], mate_r.at[4 + h])
    for d in (2, 1, 3, 0):
        s = up(up(y, d), t)
        p1a[s] = dot(gia[...], hidf[s, 0], 0, 0).astype(BF)
        p1b[:, s] = dot(gia[...], hidf[s, 1], 0, 0).astype(BF).reshape(4, 64, 256)
        if d:
            send(p1a.at[s], r1a.at[d - 1], red_s.at[0], red_r.at[0], ypeer[d])
    for d in (2, 1, 3):
        send(p1b.at[up(x, d)], r1b.at[d - 1], red_s.at[1], red_r.at[1], xpeer[d])
    for d in (2, 1, 3):
        send(p2a.at[up(y, d)], r2a.at[d - 1], red_s.at[5], red_r.at[5], ypeer[d])
        send(p2b.at[:, up(x, d)], r2b.at[d - 1], red_s.at[6], red_r.at[6], xpeer[d])

    def first(s, start):
        part = dot(gi[s], win[:, :, slab(s)].reshape(512, 512), 1, 1)
        dacc[...] = part if start else dacc[...] + part

    first(t, True)

    block_mine = up(y, t)
    wait(r1a, red_r.at[0])
    total = p1a[block_mine].astype(F32) + sum(r1a[i].astype(F32) for i in range(3))
    s1a[...] = total.astype(BF).reshape(4, 64, 256)
    for d in (2, 1, 3):
        send(s1a.at[up(x, d)], t1a.at[d - 1], red_s.at[2], red_r.at[2], xpeer[d])
    wait(r1b, red_r.at[1])
    s1b[...] = (p1b[x].astype(F32) + sum(r1b[i].astype(F32) for i in range(3))).astype(BF)
    for d in (2, 1, 3):
        send(s1b.at[up(up(y, d), t)], t1b.at[d - 1], red_s.at[3], red_r.at[3], ypeer[d])

    wait(r2a, red_r.at[5])
    s2a[...] = (p2a[y].astype(F32) + sum(r2a[i].astype(F32) for i in range(3))).astype(BF)
    wait(r2b, red_r.at[6])
    s2b[...] = (p2b[:, x].astype(F32) + sum(r2b[i].astype(F32) for i in range(3))).astype(BF)
    for d in (2, 1, 3, 0):
        for e in (0, 1):
            cc = lax.rem(c + e, 2)
            part = pl.ds(pl.multiple_of(cc * 48, 16), 48)
            xq, yq = up(x, d), up(y, d)
            if d == 0 and e == 0:
                pltpu.make_async_copy(s2a.at[x, part], t2a.at[c, x], red_r.at[7]).start()
                pltpu.make_async_copy(s2b.at[y, part], t2b.at[c, y], red_r.at[8]).start()
            else:
                k = 7 if d else 8
                send(s2a.at[xq, part], t2a.at[c, x], red_s.at[k], red_r.at[7], at(y, xq, cc))
                send(s2b.at[yq, part], t2b.at[c, y], red_s.at[k], red_r.at[8], at(yq, x, cc))

    wait(t1a, red_r.at[2])
    f1[0] = (s1a[x].astype(F32) + sum(t1a[i].astype(F32) for i in range(3))).astype(BF)
    wait(t1b, red_r.at[3])
    f1[1] = (s1b[block_mine].astype(F32) + sum(t1b[i].astype(F32) for i in range(3))).astype(BF)
    send(f1, e1.at[dp], red_s.at[4], red_r.at[4], at(*owner, dd=1 - dp))

    @pl.when(keeps)
    def _():
        pltpu.make_async_copy(f1, e1.at[dp], red_r.at[4]).start()

    @pl.when(jnp.logical_not(keeps))
    def _():
        send(f1, e1.at[dp], red_s.at[4], red_r.at[4], at(*owner))

    wait(t2a, red_r.at[7])
    wait(t2b, red_r.at[8])
    for cc in (0, 1):
        for n, f in enumerate((t2a, t2b)):
            total = sum(f[cc, i].astype(F32) for i in range(4))
            f2[:, 256 * cc + 128 * n : 256 * cc + 128 * n + 128] = total.astype(BF)
    send(f2, e2, red_s.at[9], red_r.at[9], pair)

    for d in (1, 3, 2):
        s = up(t, 4 - d)
        wait(gi.at[0], gi_r.at[d - 1])
        first(s, False)
    d_out[...] = dacc[...].astype(BF)

    for j in (0, 1):
        wait(qkv.at[j, 0, pl.ds(0, 7)], qkv_s.at[j, 0])
        for n in (0, 1):
            wait(qkv.at[j, 0, pl.ds(0, 5)], qkv_s.at[j, 1 + n])
            wait(qkv.at[j, 0, pl.ds(0, 2)], kv_s.at[j, n])
        for h in (0, 1):
            wait(osend.at[j, h, pl.ds(0, 7)], o_s.at[j, h])
    wait(wcol.at[0, :, 0], w_s.at[0])
    wait(wcol.at[0, 0, 0], w_s.at[1])
    wait(wcol.at[0, :, 0], w_s.at[2])
    wait(wcol.at[0, 0, 0], w_s.at[3])
    wait(wcol.at[pl.ds(0, 3), :, 0], w_s.at[4])
    wait(encb.at[0, pl.ds(0, 3), 0], enc_s.at[0])
    wait(encb.at[0:3, :, 0], enc_s.at[1])
    wait(encb.at[:, :, 0], enc_s.at[2])
    wait(hidf.at[pl.ds(0, 3), 0, pl.ds(0, TOK)], hid_s.at[0])
    wait(hidf.at[:, :, pl.ds(0, TOK)], mate_s.at[0])
    wait(a2.at[0:TOK], mate_s.at[1])
    for h in (0, 1):
        wait(hidf.at[pl.ds(0, 3), 1, pl.ds(0, 64)], hid_s.at[1 + h])
        wait(tgt.at[h, pl.ds(0, 3)], tg_s.at[h])
        wait(precv.at[h], p_s.at[h])
        wait(g2.at[0:48], g_s.at[h])
        wait(g2.at[0:64], mate_s.at[2 + h])
        wait(gia.at[0:64], mate_s.at[4 + h])
    wait(gi.at[pl.ds(0, 3)], gi_s)
    wait(r1a, red_s.at[0])
    wait(r1b, red_s.at[1])
    wait(t1a, red_s.at[2])
    wait(t1b, red_s.at[3])
    wait(r2a, red_s.at[5])
    wait(r2b, red_s.at[6])
    wait(r2a.at[:, pl.ds(0, 2)], red_s.at[7])
    wait(s2a.at[0], red_s.at[8])
    wait(f2, red_s.at[9])

    @pl.when(keeps)
    def _():
        wait(f1, red_s.at[4])

    @pl.when(jnp.logical_not(keeps))
    def _():
        wait(e1, red_s.at[4])

    wait(e2, red_r.at[9])
    gout_out[...] = f2[...].astype(F32) + e2[...].astype(F32)
    wait(e1, red_r.at[4])
    for j in (0, 1):
        total = e1[0, j].astype(F32) + e1[1, j].astype(F32)
        for cc in (0, 1):
            lo = (2 * cc + j) * HD
            gin_out[:, lo : lo + HD] = total[:, cc * HD : cc * HD + HD]


def keep(a, b, c, a_out, b_out, c_out):
    a_out[...] = a[...]
    b_out[...] = b[...]
    c_out[...] = c[...]


def local(
    residual, queries, attn_keys, attn_values, gate_table, timesteps, enc_feats,
    tap_rows, tap_weights, proj_in, proj_out,
):
    dma = pltpu.SemaphoreType.DMA
    vm = pl.BlockSpec(memory_space=VMEM)
    hb = pl.BlockSpec(memory_space=pl.ANY)
    sm = pl.BlockSpec(memory_space=pltpu.SMEM)
    d_hidden, gin, gout = pl.pallas_call(
        kernel,
        name="alignment",
        out_shape=(
            jax.ShapeDtypeStruct((TOK, 512), BF),
            jax.ShapeDtypeStruct((64, 512), F32),
            jax.ShapeDtypeStruct((48, 512), F32),
        ),
        in_specs=[vm, hb, hb, hb, hb, sm, hb, vm, vm, hb, hb],
        out_specs=(vm, vm, vm),
        scratch_shapes=[
            VMEM((2, 3, 8, TOK, HD), BF),
            VMEM((1000, 512), BF),
            VMEM((4, HD, 2048), BF),
            VMEM((4, 2, 2, HD, 512), BF),
            VMEM((512, 1536), BF),
            VMEM((4, 4, 2, 48, 384), BF),
            VMEM((2, 2, 8, 80, HD), BF),
            VMEM((2, 4, 2, 2, 80, HD), BF),
            VMEM((2, 8 * TOK, 256), F32),
            VMEM((2, 8, 256), F32),
            VMEM((TOK, 384), BF),
            VMEM((2, 4, 16, 384), BF),
            VMEM((4, 2, 2 * TOK, 256), BF),
            VMEM((TOK, 512), F32),
            VMEM((TOK, 512), BF),
            VMEM((2 * TOK, 256), BF),
            VMEM((TOK, 1536), BF),
            VMEM((2, 3, 16, 1536), BF),
            VMEM((2 * TOK, 1536), BF),
            VMEM((4, TOK, 512), BF),
            VMEM((2 * TOK, 256), BF),
            VMEM((TOK, 512), F32),
            VMEM((4, 256, 256), BF),
            VMEM((4, 4, 64, 256), BF),
            VMEM((3, 256, 256), BF),
            VMEM((3, 4, 64, 256), BF),
            VMEM((4, 64, 256), BF),
            VMEM((4, 64, 256), BF),
            VMEM((3, 64, 256), BF),
            VMEM((3, 64, 256), BF),
            VMEM((2, 64, 256), BF),
            VMEM((2, 2, 64, 256), BF),
            VMEM((4, 4, 96, 128), BF),
            VMEM((4, 4, 96, 128), BF),
            VMEM((3, 4, 96, 128), BF),
            VMEM((3, 4, 96, 128), BF),
            VMEM((4, 96, 128), BF),
            VMEM((4, 96, 128), BF),
            VMEM((2, 4, 48, 128), BF),
            VMEM((2, 4, 48, 128), BF),
            VMEM((48, 512), BF),
            VMEM((48, 512), BF),
            dma((5,)),
            dma((2, 3)),
            dma((2, 3)),
            dma((2, 2)),
            dma((2, 2)),
            dma((5,)),
            dma((5,)),
            dma((3,)),
            dma((3,)),
            dma((2, 2)),
            dma((2, 2)),
            dma((2,)),
            dma((2,)),
            dma((6,)),
            dma((6,)),
            dma((3,)),
            dma((3,)),
            dma((2,)),
            dma((2,)),
            dma((2,)),
            dma((2,)),
            dma,
            dma((3,)),
            dma((10,)),
            dma((10,)),
        ],
        compiler_params=pltpu.CompilerParams(
            collective_id=0, has_side_effects=True, vmem_limit_bytes=56 << 20
        ),
        cost_estimate=pl.CostEstimate(
            flops=2_500_000_000, bytes_accessed=16_000_000, transcendentals=2_200_000
        ),
    )(
        residual[0], queries[0], attn_keys[0], attn_values[0], gate_table, timesteps,
        enc_feats[0], tap_rows[0].T, tap_weights[0].T, proj_in.reshape(4, HD, 2048), proj_out,
    )
    d_hidden, gin, gout = pl.pallas_call(
        keep,
        name="keep",
        out_shape=(
            jax.ShapeDtypeStruct((TOK, 512), BF),
            jax.ShapeDtypeStruct((64, 512), F32),
            jax.ShapeDtypeStruct((48, 512), F32),
        ),
        in_specs=[vm, vm, vm],
        out_specs=(vm, vm, vm),
    )(d_hidden, gin, gout)
    return d_hidden[None], gin.T, gout.T


def solution(mesh):
    in_specs = (
        P("dp", "ctx", "tp"),
        P("dp", "ctx", "tp"),
        P("dp", "ctx", "tp"),
        P("dp", "ctx", "tp"),
        P(None, "tp"),
        P("dp"),
        P("dp", "ctx", "tp"),
        P("dp", "ctx", None),
        P("dp", "ctx", None),
        P("tp", None),
        P("tp", None),
    )
    out_specs = (P("dp", "ctx", "tp"), P("tp", "ctx"), P("tp", "ctx"))
    return jax.shard_map(local, mesh=mesh, in_specs=in_specs, out_specs=out_specs, check_vma=False)
```
